32 devices in a mesh: parts: 2 (over y), own: 16 (over z, x, core).
Axes of the slice: x: 2, y: 2, z: 4, core: 2. Of those that a mesh axis runs over, the one named last changes fastest.
Arguments:
- amplitudes: bfloat16 [128, 1024, 256], P(('parts', 'own')), parts along dimension 0, may hold values from -6 to 6
- integrals: bfloat16 [1536, 256, 256], P(('parts', 'own')), parts along dimension 0, may hold values from -0.375 to 0.375
- tasks: int32 [1536, 2], P(('parts', 'own')), parts along dimension 0, may hold values from 0 to 63, as said below
Outputs:
- residual: float32 [128, 1024, 256], P(('parts', 'own')), parts along dimension 0
The draws below stay inside these ranges and needn't reach their ends.
There are 2 independent parts, one for each index of `parts`. The reference program is written for one: setup_inputs(seed, part) draws one part's arguments, and reference() takes and returns one part's arrays. A program takes and returns all parts, laid end to end along the dimension named above; each array names one. Nothing has to cross between parts.
Inputs may be any that keep to these rules, and one draw needn't show every extreme that they name: `tasks`: task k stored on group g = k // 48 has source and target tiles in g * 4 - 2 to (g + 1) * 4 + 1; the first task of each group has the lowest such source, the second the highest; the third targets the tile just below the group's own and the fourth the tile just above, where such tiles exist.
All inputs are finite; a program needn't handle non-finite values.
Results may differ from the reference program's by a relative error of at most 0.0021.
Values may be sent and summed in bfloat16 or wider, within the bound.
No kernel may reach another device: no remote copies, remote signals or barrier semaphores. Data moves between devices by JAX's collectives and lax.ppermute only.
A program may use at most 256 MiB of HBM per device.

```python
import jax
import jax.numpy as jnp
from jax import lax

W = 256
ROWS = 1024
TILE_DEV = 4
TASK_DEV = 48
HALO = 2
NT = 64
NTASK = 768
N_OWN = 16


def draw_tasks(key, part):
    key = jax.random.fold_in(key, 11)
    key_source, key_target = jax.random.split(key)
    position = jnp.arange(NTASK, dtype=jnp.int32)
    device_id = position // TASK_DEV
    slot_id = position % TASK_DEV
    lowest = jnp.maximum(device_id * TILE_DEV - HALO, 0)
    highest = jnp.minimum(device_id * TILE_DEV + TILE_DEV + HALO, NT)
    extent = highest - lowest
    source = lowest + jax.random.randint(key_source, (NTASK,), 0, 1 << 20, dtype=jnp.int32) % extent
    target = lowest + jax.random.randint(key_target, (NTASK,), 0, 1 << 20, dtype=jnp.int32) % extent
    source = jnp.where(slot_id == 0, lowest, source)
    source = jnp.where(slot_id == 1, highest - 1, source)
    below = device_id * TILE_DEV - 1
    above = device_id * TILE_DEV + TILE_DEV
    target = jnp.where((slot_id == 2) & (below >= 0), below, target)
    target = jnp.where((slot_id == 3) & (above < NT), above, target)
    return jnp.stack([source, target], axis=1).astype(jnp.int32)


def block_levels(stream_key, shape, shards, low, high):
    def one(dim, parts):
        steps = jax.random.uniform(jax.random.fold_in(jax.random.fold_in(stream_key, 6), dim), (parts,), jnp.float32, low / len(shards), high / len(shards))
        return jnp.repeat(jnp.exp(steps), shape[dim] // parts).reshape((-1,) + (1,) * (len(shape) - dim - 1))

    loudness = one(*shards[0])
    for cut in shards[1:]:
        loudness = loudness * one(*cut)
    return loudness


def scatter_about(own_key, shape, scale, limit, cuts=(), kind=jnp.bfloat16):
    array = scale * jax.random.normal(own_key, shape, jnp.float32)
    if cuts:
        array = array * block_levels(own_key, shape, cuts, -0.22, 0.18)
    return jnp.clip(array, -limit, limit).astype(kind)


def setup_inputs(seed: int = 0, part: int = 0) -> dict:
    splits = jax.random.split(jax.random.key(seed), 4)
    part_splits = jax.random.split(jax.random.fold_in(splits[3], part), 4)
    return {
        "amplitudes": scatter_about(part_splits[0], (NT, ROWS, W), 1.0, 6.0, ((0, 16),)),
        "integrals": scatter_about(part_splits[1], (NTASK, W, W), W ** -0.5, 0.375, ((0, 16),)),
        "tasks": draw_tasks(jax.random.fold_in(jax.random.fold_in(splits[3], part), 71), part),
    }


def reference(amplitudes, integrals, tasks):
    tile_count = amplitudes.shape[0]
    extent = TILE_DEV + 2 * HALO
    padded = jnp.pad(amplitudes, ((HALO, HALO), (0, 0), (0, 0)))
    blocks_v = integrals.reshape(N_OWN, TASK_DEV, W, W)
    blocks_t = tasks.reshape(N_OWN, TASK_DEV, 2)

    def accumulate(running, payload):
        device_id, block_v, block_t = payload
        first_tile = (device_id * TILE_DEV).astype(jnp.int32)
        picked = jnp.take(padded, block_t[:, 0] + HALO, axis=0)
        products = jnp.einsum("krw,kwv->krv", picked.astype(jnp.float32), block_v.astype(jnp.float32))
        target = (block_t[:, 1] - first_tile + HALO).astype(jnp.int32)
        summed = jax.ops.segment_sum(products, target, num_segments=extent)
        low_rim = lax.optimization_barrier(summed[:HALO].astype(jnp.bfloat16)).astype(jnp.float32)
        high_rim = lax.optimization_barrier(summed[HALO + TILE_DEV:].astype(jnp.bfloat16)).astype(jnp.float32)
        pieces = jnp.concatenate([low_rim, summed[HALO:HALO + TILE_DEV], high_rim], axis=0)
        current = lax.dynamic_slice_in_dim(running, first_tile, extent, 0)
        running = lax.dynamic_update_slice_in_dim(running, current + pieces, first_tile, 0)
        return running, None

    start = jnp.zeros((tile_count + 2 * HALO, ROWS, W), jnp.float32)
    running, _ = lax.scan(accumulate, start, (jnp.arange(N_OWN, dtype=jnp.int32), blocks_v, blocks_t))
    return running[HALO:HALO + tile_count]
```

```python
import functools

import jax
import jax.numpy as jnp
from jax import lax
from jax.experimental import pallas as pl
from jax.experimental.pallas import tpu as pltpu
from jax.sharding import PartitionSpec as P

HALO = 2
SPLIT = (512, 512)
VMEM_LIMIT = 24 * 1024 * 1024

OWN, CHIP, CROSS = 0, 1, 2
LISTS = 6


def row_chunks(rows):
    total = sum(SPLIT)
    sizes = [rows * part // total for part in SPLIT]
    starts = [sum(sizes[:i]) for i in range(len(sizes))]
    return list(zip(starts, sizes))


def vmem():
    return pl.BlockSpec(memory_space=pltpu.VMEM)


def smem():
    return pl.BlockSpec(memory_space=pltpu.SMEM)


def in_vmem(x):
    return pltpu.with_memory_space_constraint(x, pltpu.VMEM)


def accumulate(plan, which, source, rows, integrals, sums):
    start, size = rows

    def one(i, carry):
        entry = plan[which, i]
        task = entry >> 8
        src = (entry >> 4) & 15
        dst = entry & 15
        sums[dst] += jnp.dot(
            source[src, pl.ds(start, size)],
            integrals[task],
            preferred_element_type=jnp.float32,
        )
        return carry

    lax.fori_loop(0, plan[which, plan.shape[1] - 1], one, 0)


def make_plan(axis, tile_count, tasks, plan):
    me = lax.axis_index(axis)
    odd = lax.rem(me, 2)
    first = me * tile_count
    last = plan.shape[1] - 1
    for which in range(LISTS):
        plan[which, last] = 0
    plan[LISTS, 0] = odd

    def place(tile):
        own = tile - first
        below = own < 0
        above = own >= tile_count
        low = own + HALO
        high = own - tile_count
        outside = jnp.logical_or(below, above)
        crossing = jnp.logical_or(
            jnp.logical_and(below, odd == 0), jnp.logical_and(above, odd == 1)
        )
        slot = jnp.where(below, low, jnp.where(above, high, own))
        kind = jnp.where(crossing, CROSS, jnp.where(outside, CHIP, OWN))
        return slot, kind

    def one(k, carry):
        src, src_kind = place(tasks[k, 0])
        dst, dst_kind = place(tasks[k, 1])
        dst = dst + jnp.where(dst_kind == CHIP, tile_count, 0)
        which = 2 * src_kind + jnp.where(dst_kind == CROSS, 1, 0)
        count = plan[which, last]
        plan[which, count] = k * 256 + src * 16 + dst
        plan[which, last] = count + 1
        return carry

    lax.fori_loop(0, tasks.shape[0], one, 0)


def first_kernel(axis, chunks, tasks, own, chip, integrals, plan, *sums):
    make_plan(axis, own.shape[0], tasks, plan)
    crossing, staying = sums[: len(chunks)], sums[len(chunks) :]
    for ref in sums:
        ref[...] = jnp.zeros_like(ref)
    for rows, out_cross, out_stay in zip(chunks, crossing, staying):
        accumulate(plan, 2 * OWN + 1, own, rows, integrals, out_cross)
        accumulate(plan, 2 * OWN, own, rows, integrals, out_stay)
        accumulate(plan, 2 * CHIP + 1, chip, rows, integrals, out_cross)
        accumulate(plan, 2 * CHIP, chip, rows, integrals, out_stay)


def cross_kernel(plan, halo, integrals, sums, rim, total):
    total[...] = sums[...]
    accumulate(plan, 2 * CROSS + 1, halo, (0, halo.shape[1]), integrals, total)
    rim[...] = total[...].astype(rim.dtype)


def stay_kernel(plan, halo, integrals, sums, resident, rim, total):
    total[...] = sums[...]
    accumulate(plan, 2 * CROSS, halo, (0, halo.shape[1]), integrals, total)
    kept = resident.shape[0]
    resident[...] = total[:kept]
    rim[...] = total[kept:].astype(rim.dtype)


def last_kernel(chunks, plan, *refs):
    count = len(chunks)
    resident, cross, chip = refs[:count], refs[count : 2 * count], refs[2 * count : 3 * count]
    out = refs[-1]
    odd = plan[LISTS, 0]
    edge = out.shape[0] - HALO
    for (start, size), kept, from_cross, from_chip in zip(chunks, resident, cross, chip):
        rows = pl.ds(start, size)
        for j in range(HALO):
            near = odd * edge + j
            far = (1 - odd) * edge + j
            out[near, rows] = kept[near] + from_cross[j].astype(jnp.float32)
            out[far, rows] = kept[far] + from_chip[j].astype(jnp.float32)


def params():
    return pltpu.CompilerParams(vmem_limit_bytes=VMEM_LIMIT)


def cost(flops, nbytes):
    return pl.CostEstimate(flops=int(flops), bytes_accessed=int(nbytes), transcendentals=0)


def on_device(amplitudes, integrals, tasks):
    tile_count, rows, width = amplitudes.shape
    task_count = integrals.shape[0]
    chunks = row_chunks(rows)
    sizes = [size for _, size in chunks]
    axis = "own"
    devices = lax.axis_size(axis)
    cross_pairs = [(i, i + 1) for i in range(1, devices - 1, 2)]
    cross_pairs += [(b, a) for a, b in cross_pairs]
    chip_pairs = [(i, i ^ 1) for i in range(devices)]
    odd = lax.rem(lax.axis_index(axis), 2)
    edge = tile_count - HALO
    near, far = odd * edge, (1 - odd) * edge
    f32, bf16 = jnp.float32, amplitudes.dtype

    def swap_cross(x):
        return lax.ppermute(x, axis, cross_pairs)

    def swap_chip(x):
        return lax.ppermute(x, axis, chip_pairs)

    zero = jnp.int32(0)
    cross_halo = [
        swap_cross(lax.dynamic_slice(amplitudes, (near, jnp.int32(start), zero), (HALO, size, width)))
        for start, size in chunks
    ]
    chip_halo = swap_chip(lax.dynamic_slice(amplitudes, (far, zero, zero), (HALO, rows, width)))

    here = in_vmem(integrals)
    flops = 2 * rows * width * width
    plan, *sums = pl.pallas_call(
        functools.partial(first_kernel, axis, chunks),
        out_shape=[jax.ShapeDtypeStruct((LISTS + 1, task_count + 1), jnp.int32)]
        + [pltpu.VMEM((HALO, size, width), f32) for size in sizes]
        + [pltpu.VMEM((tile_count + HALO, size, width), f32) for size in sizes],
        in_specs=[smem(), vmem(), vmem(), vmem()],
        out_specs=[smem()] + [vmem()] * (2 * len(chunks)),
        compiler_params=params(),
        cost_estimate=cost(flops * task_count, 20 << 20),
        name="chip_sources",
    )(tasks, in_vmem(amplitudes), in_vmem(chip_halo), here)
    cross_sums, stay_sums = sums[: len(chunks)], sums[len(chunks) :]

    resident, from_cross, from_chip = [], [], []
    for size, halo, cross_sum, stay_sum in zip(sizes, cross_halo, cross_sums, stay_sums):
        share = flops * size // rows
        halo = in_vmem(halo)
        rim = pl.pallas_call(
            cross_kernel,
            out_shape=pltpu.VMEM((HALO, size, width), bf16),
            in_specs=[smem(), vmem(), vmem(), vmem()],
            out_specs=vmem(),
            scratch_shapes=[pltpu.VMEM((HALO, size, width), f32)],
            compiler_params=params(),
            cost_estimate=cost(share * 6, 4 << 20),
            name="cross_rim",
        )(plan, halo, here, in_vmem(cross_sum))
        from_cross.append(swap_cross(rim))
        kept, rim = pl.pallas_call(
            stay_kernel,
            out_shape=[
                pltpu.VMEM((tile_count, size, width), f32),
                pltpu.VMEM((HALO, size, width), bf16),
            ],
            in_specs=[smem(), vmem(), vmem(), vmem()],
            out_specs=[vmem()] * 2,
            scratch_shapes=[pltpu.VMEM((tile_count + HALO, size, width), f32)],
            compiler_params=params(),
            cost_estimate=cost(share * 12, 4 << 20),
            name="chip_rim",
        )(plan, halo, here, in_vmem(stay_sum))
        resident.append(in_vmem(kept))
        from_chip.append(swap_chip(rim))

    return pl.pallas_call(
        functools.partial(last_kernel, chunks),
        out_shape=jax.ShapeDtypeStruct((tile_count, rows, width), f32),
        in_specs=[smem()] + [vmem()] * (3 * len(chunks)),
        out_specs=vmem(),
        compiler_params=params(),
        cost_estimate=cost(0, 10 << 20),
        name="residual",
    )(plan, *resident, *[in_vmem(x) for x in from_cross], *[in_vmem(x) for x in from_chip])


def solution(mesh):
    return jax.shard_map(
        on_device,
        mesh=mesh,
        in_specs=(
            P(("parts", "own"), None, None),
            P(("parts", "own"), None, None),
            P(("parts", "own"), None),
        ),
        out_specs=P(("parts", "own"), None, None),
        check_vma=False,
    )
```

```python
import functools

import jax
import jax.numpy as jnp
from jax import lax
from jax.experimental import pallas as pl
from jax.experimental.pallas import tpu as pltpu
from jax.sharding import PartitionSpec as P

HALO = 2
SPLIT = (512, 512)
CHIP_SPLIT = (384, 384, 256)
VMEM_LIMIT = 24 * 1024 * 1024

OWN, CHIP, CROSS = 0, 1, 2
LISTS = 6


def row_chunks(rows, split):
    total = sum(split)
    sizes = [rows * part // total for part in split]
    starts = [sum(sizes[:i]) for i in range(len(sizes))]
    return list(zip(starts, sizes))


def vmem():
    return pl.BlockSpec(memory_space=pltpu.VMEM)


def smem():
    return pl.BlockSpec(memory_space=pltpu.SMEM)


def hbm():
    return pl.BlockSpec(memory_space=pltpu.HBM)


def in_vmem(x):
    return pltpu.with_memory_space_constraint(x, pltpu.VMEM)


def in_hbm(x):
    return pltpu.with_memory_space_constraint(x, pltpu.HBM)


def accumulate(plan, which, source, integrals, sums, rows=None):
    start, size = rows or (0, source.shape[1])
    offset = 0 if sums.shape[1] == size else start
    begin = 0 if source.shape[1] == size else start
    block = 256 if size % 256 == 0 else 128
    count = plan[which, plan.shape[1] - 1]

    def some(first, width):
        entries = [plan[which, first + u] for u in range(width)]
        for r in range(0, size, block):
            products = [
                jnp.dot(
                    source[(entry >> 4) & 15, pl.ds(begin + r, block)],
                    integrals[entry >> 8],
                    preferred_element_type=jnp.float32,
                )
                for entry in entries
            ]
            for entry, product in zip(entries, products):
                sums[entry & 15, pl.ds(offset + r, block)] += product

    def pair(i, carry):
        some(2 * i, 2)
        return carry

    def single(i, carry):
        some(i, 1)
        return carry

    pairs = count // 2
    lax.fori_loop(0, pairs, pair, 0)
    lax.fori_loop(2 * pairs, count, single, 0)


def make_plan(axis, tile_count, tasks, plan):
    odd = lax.rem(lax.axis_index(axis), 2)
    first = lax.axis_index(axis) * tile_count
    last = plan.shape[1] - 1
    for which in range(LISTS):
        plan[which, last] = 0
    plan[LISTS, 0] = odd

    def place(tile):
        own = tile - first
        below = own < 0
        above = own >= tile_count
        crossing = jnp.logical_or(
            jnp.logical_and(below, odd == 0), jnp.logical_and(above, odd == 1)
        )
        slot = jnp.where(below, own + HALO, jnp.where(above, own - tile_count, own))
        kind = jnp.where(crossing, CROSS, jnp.where(jnp.logical_or(below, above), CHIP, OWN))
        return slot, kind

    def one(k, carry):
        src, src_kind = place(tasks[0, k])
        dst, dst_kind = place(tasks[1, k])
        dst = dst + jnp.where(dst_kind == CHIP, tile_count, 0)
        which = 2 * src_kind + jnp.where(dst_kind == CROSS, 1, 0)
        count = plan[which, last]
        plan[which, count] = k * 256 + src * 16 + dst
        plan[which, last] = count + 1
        return carry

    lax.fori_loop(0, tasks.shape[1], one, 0)


def edges(odd, tile_count):
    edge = tile_count - HALO
    return odd * edge, (1 - odd) * edge


def pick_kernel(axis, chunks, amplitudes, *refs):
    *picked, sems = refs
    near, far = edges(lax.rem(lax.axis_index(axis), 2), amplitudes.shape[0])
    copies = [
        pltpu.make_async_copy(
            amplitudes.at[pl.ds(near, HALO), pl.ds(start, size)], picked[i], sems.at[i]
        )
        for i, (start, size) in enumerate(chunks)
    ]
    i = len(chunks)
    copies.append(
        pltpu.make_async_copy(amplitudes.at[pl.ds(far, HALO)], picked[i], sems.at[i])
    )
    for copy in copies:
        copy.start()
    for copy in copies:
        copy.wait()


def first_kernel(axis, chunks, tasks, amplitudes, chip, integrals, plan, own, held, *refs):
    *sums, sems = refs
    copies = [
        pltpu.make_async_copy(amplitudes, own, sems.at[0]),
        pltpu.make_async_copy(integrals, held, sems.at[1]),
    ]
    for copy in copies:
        copy.start()
    make_plan(axis, amplitudes.shape[0], tasks, plan)
    for ref in sums:
        ref[...] = jnp.zeros_like(ref)
    for copy in copies:
        copy.wait()
    for rows, total in zip(chunks, sums):
        accumulate(plan, 2 * OWN + 1, own, held, total, rows)
        accumulate(plan, 2 * CHIP + 1, chip, held, total, rows)


def own_kernel(plan, own, integrals, sums):
    sums[...] = jnp.zeros_like(sums)
    accumulate(plan, 2 * OWN, own, integrals, sums)


def cross_kernel(plan, halo, integrals, sums, rim, total):
    accumulate(plan, 2 * CROSS + 1, halo, integrals, total)
    rim[...] = total[...].astype(rim.dtype)


def stay_kernel(rows, plan, halo, integrals, sums, total):
    accumulate(plan, 2 * CROSS, halo, integrals, total, rows)


def chip_kernel(rows, chip_chunks, plan, halo, chip, integrals, sums, total, *rims):
    accumulate(plan, 2 * CROSS, halo, integrals, total, rows)
    accumulate(plan, 2 * CHIP, chip, integrals, total)
    for (start, size), rim in zip(chip_chunks, rims):
        rim[...] = total[total.shape[0] - HALO :, pl.ds(start, size)].astype(rim.dtype)


def rest_kernel(chunks, chip_chunks, plan, sums, *refs):
    chip, cross = refs[: len(chip_chunks)], refs[len(chip_chunks) : -3]
    out, whole, sems = refs[-3:]
    near, far = edges(plan[LISTS, 0], out.shape[0])
    copies = []
    for j in range(HALO):
        for (start, size), rim in zip(chip_chunks, chip):
            rows = pl.ds(start, size)
            whole[j, rows] = sums[far + j, rows] + rim[j].astype(jnp.float32)
        copies.append(pltpu.make_async_copy(whole.at[j], out.at[far + j], sems.at[j]))
        copies[-1].start()
    done = pl.ds(0, chunks[-1][0])
    for j in range(HALO):
        for (start, size), rim in zip(chunks[:-1], cross):
            rows = pl.ds(start, size)
            whole[HALO + j, rows] = sums[near + j, rows] + rim[j].astype(jnp.float32)
        copies.append(
            pltpu.make_async_copy(
                whole.at[HALO + j, done], out.at[near + j, done], sems.at[HALO + j]
            )
        )
        copies[-1].start()
    for copy in copies:
        copy.wait()


def last_kernel(rows, plan, sums, rim, before, out, part, sems):
    near, _ = edges(plan[LISTS, 0], out.shape[0])
    rows = pl.ds(*rows)
    copies = []
    for j in range(HALO):
        part[j] = sums[near + j, rows] + rim[j].astype(jnp.float32)
        copies.append(pltpu.make_async_copy(part.at[j], out.at[near + j, rows], sems.at[j]))
        copies[-1].start()
    for copy in copies:
        copy.wait()


def on_device(amplitudes, integrals, tasks):
    tile_count, rows, width = amplitudes.shape
    task_count = integrals.shape[0]
    chunks = row_chunks(rows, SPLIT)
    chip_chunks = row_chunks(rows, CHIP_SPLIT)
    sizes = [size for _, size in chunks]
    count = len(chunks)
    axis = "own"
    devices = lax.axis_size(axis)
    cross_pairs = [(i, i + 1) for i in range(1, devices - 1, 2)]
    cross_pairs += [(b, a) for a, b in cross_pairs]
    chip_pairs = [(i, i ^ 1) for i in range(devices)]
    f32, bf16, i32 = jnp.float32, amplitudes.dtype, jnp.int32

    def call(kernel, name, operands, in_specs, after=(), **kwargs):
        here = len(operands)

        def body(*refs):
            kernel(*refs[:here], *refs[here + len(after) :])

        return pl.pallas_call(
            body,
            in_specs=in_specs + [pl.BlockSpec(memory_space=pl.ANY)] * len(after),
            compiler_params=pltpu.CompilerParams(vmem_limit_bytes=VMEM_LIMIT),
            cost_estimate=pl.CostEstimate(flops=1, bytes_accessed=1, transcendentals=0),
            name=name,
            **kwargs,
        )(*operands, *after)

    def swap_cross(x):
        return in_vmem(lax.ppermute(x, axis, cross_pairs))

    def swap_chip(x):
        return in_vmem(lax.ppermute(x, axis, chip_pairs))

    amplitudes, integrals = in_hbm(amplitudes), in_hbm(integrals)
    picked = call(
        functools.partial(pick_kernel, axis, chunks),
        "pick",
        [amplitudes],
        [hbm()],
        out_shape=[jax.ShapeDtypeStruct((HALO, size, width), bf16) for size in sizes + [rows]],
        out_specs=[hbm()] * (count + 1),
        scratch_shapes=[pltpu.SemaphoreType.DMA((count + 1,))],
    )
    cross_halo = [swap_cross(x) for x in picked[:count]]
    chip_halo = swap_chip(picked[count])

    plan, own, held, *cross_sums = call(
        functools.partial(first_kernel, axis, chunks),
        "cross_targets",
        [tasks.T, amplitudes, chip_halo, integrals],
        [smem(), hbm(), vmem(), hbm()],
        out_shape=[
            jax.ShapeDtypeStruct((LISTS + 1, task_count + 1), i32),
            pltpu.VMEM(amplitudes.shape, bf16),
            pltpu.VMEM(integrals.shape, bf16),
        ]
        + [pltpu.VMEM((HALO, size, width), f32) for size in sizes],
        out_specs=[smem()] + [vmem()] * (count + 2),
        scratch_shapes=[pltpu.SemaphoreType.DMA((2,))],
    )
    own, held = in_vmem(own), in_vmem(held)
    whole = pltpu.VMEM((tile_count + HALO, rows, width), f32)
    sums = call(
        own_kernel,
        "own_sources",
        [plan, own, held],
        [smem()] + [vmem()] * 2,
        out_shape=whole,
        out_specs=vmem(),
    )

    from_cross = []
    for chunk, halo, cross_sum in zip(chunks, cross_halo, cross_sums):
        size = chunk[1]
        rim, _ = call(
            cross_kernel,
            "cross_rim",
            [plan, halo, held, in_vmem(cross_sum)],
            [smem()] + [vmem()] * 3,
            after=[in_vmem(sums)],
            out_shape=[
                pltpu.VMEM((HALO, size, width), bf16),
                pltpu.VMEM((HALO, size, width), f32),
            ],
            out_specs=[vmem()] * 2,
            input_output_aliases={3: 1},
        )
        from_cross.append(swap_cross(rim))
        if len(from_cross) < count:
            sums = call(
                functools.partial(stay_kernel, chunk),
                "cross_sources",
                [plan, halo, held, in_vmem(sums)],
                [smem()] + [vmem()] * 3,
                after=[rim],
                out_shape=whole,
                out_specs=vmem(),
                input_output_aliases={3: 0},
            )
    sums, *rims = call(
        functools.partial(chip_kernel, chunks[-1], chip_chunks),
        "chip_rim",
        [plan, cross_halo[-1], chip_halo, held, in_vmem(sums)],
        [smem()] + [vmem()] * 4,
        after=[rim],
        out_shape=[whole] + [pltpu.VMEM((HALO, size, width), bf16) for _, size in chip_chunks],
        out_specs=[vmem()] * (1 + len(chip_chunks)),
        input_output_aliases={4: 0},
    )
    from_chip = [swap_chip(x) for x in rims]

    sums = in_vmem(sums)
    shape = jax.ShapeDtypeStruct((tile_count, rows, width), f32)
    out = call(
        functools.partial(rest_kernel, chunks, chip_chunks),
        "residual",
        [plan, sums, *from_chip, *from_cross[:-1]],
        [smem()] + [vmem()] * (count + len(chip_chunks)),
        out_shape=shape,
        out_specs=hbm(),
        scratch_shapes=[
            pltpu.VMEM((2 * HALO, rows, width), f32),
            pltpu.SemaphoreType.DMA((2 * HALO,)),
        ],
    )
    return call(
        functools.partial(last_kernel, chunks[-1]),
        "residual_last",
        [plan, sums, from_cross[-1], out],
        [smem()] + [vmem()] * 2 + [hbm()],
        out_shape=shape,
        out_specs=hbm(),
        scratch_shapes=[
            pltpu.VMEM((HALO, sizes[-1], width), f32),
            pltpu.SemaphoreType.DMA((HALO,)),
        ],
        input_output_aliases={3: 0},
    )


def solution(mesh):
    return jax.shard_map(
        on_device,
        mesh=mesh,
        in_specs=(
            P(("parts", "own"), None, None),
            P(("parts", "own"), None, None),
            P(("parts", "own"), None),
        ),
        out_specs=P(("parts", "own"), None, None),
        check_vma=False,
    )
```

```python
import functools

import jax
import jax.numpy as jnp
from jax import lax
from jax.experimental import pallas as pl
from jax.experimental.pallas import tpu as pltpu
from jax.sharding import PartitionSpec as P

HALO = 2
SPLIT = (512, 512)
CHIP_SPLIT = (352, 352, 320)
VMEM_LIMIT = 24 * 1024 * 1024

OWN, CHIP, CROSS = 0, 1, 2
LISTS = 9


def row_chunks(rows, split):
    total = sum(split)
    sizes = [rows * part // total for part in split]
    starts = [sum(sizes[:i]) for i in range(len(sizes))]
    return list(zip(starts, sizes))


def vmem():
    return pl.BlockSpec(memory_space=pltpu.VMEM)


def smem():
    return pl.BlockSpec(memory_space=pltpu.SMEM)


def hbm():
    return pl.BlockSpec(memory_space=pltpu.HBM)


def in_vmem(x):
    return pltpu.with_memory_space_constraint(x, pltpu.VMEM)


def in_hbm(x):
    return pltpu.with_memory_space_constraint(x, pltpu.HBM)


def accumulate(plan, which, source, begin, integrals, sums, offset, size):
    blocks = [(r, min(256, size - r)) for r in range(0, size, 256)]
    count = plan[which, plan.shape[1] - 1]

    def some(first, width):
        entries = [plan[which, first + u] for u in range(width)]
        for r, block in blocks:
            products = [
                jnp.dot(
                    source[(entry >> 4) & 15, pl.ds(begin + r, block)],
                    integrals[entry >> 8],
                    preferred_element_type=jnp.float32,
                )
                for entry in entries
            ]
            for entry, product in zip(entries, products):
                sums[entry & 15, pl.ds(offset + r, block)] += product

    def pair(i, carry):
        some(2 * i, 2)
        return carry

    def single(i, carry):
        some(i, 1)
        return carry

    pairs = count // 2
    lax.fori_loop(0, pairs, pair, 0)
    lax.fori_loop(2 * pairs, count, single, 0)


def make_plan(axis, tile_count, tasks, plan):
    odd = lax.rem(lax.axis_index(axis), 2)
    first = lax.axis_index(axis) * tile_count
    last = plan.shape[1] - 1
    for which in range(LISTS):
        plan[which, last] = 0

    def place(tile):
        own = tile - first
        below = own < 0
        above = own >= tile_count
        crossing = jnp.logical_or(
            jnp.logical_and(below, odd == 0), jnp.logical_and(above, odd == 1)
        )
        slot = jnp.where(below, own + HALO, jnp.where(above, own - tile_count, own))
        kind = jnp.where(crossing, CROSS, jnp.where(jnp.logical_or(below, above), CHIP, OWN))
        return slot, kind

    def one(k, carry):
        src, src_kind = place(tasks[0, k])
        dst, dst_kind = place(tasks[1, k])
        which = 3 * src_kind + dst_kind
        count = plan[which, last]
        plan[which, count] = k * 256 + src * 16 + dst
        plan[which, last] = count + 1
        return carry

    lax.fori_loop(0, tasks.shape[1], one, 0)


def edges(axis, tile_count):
    odd = lax.rem(lax.axis_index(axis), 2)
    edge = tile_count - HALO
    return odd * edge, (1 - odd) * edge


def pick_kernel(axis, chunks, amplitudes, *refs):
    *picked, sems = refs
    near, far = edges(axis, amplitudes.shape[0])
    copies = [
        pltpu.make_async_copy(
            amplitudes.at[pl.ds(near, HALO), pl.ds(start, size)], picked[i], sems.at[i]
        )
        for i, (start, size) in enumerate(chunks)
    ]
    i = len(chunks)
    copies.append(
        pltpu.make_async_copy(amplitudes.at[pl.ds(far, HALO)], picked[i], sems.at[i])
    )
    for copy in copies:
        copy.start()
    for copy in copies:
        copy.wait()


def first_kernel(axis, chunks, tasks, amplitudes, integrals, chip, *refs):
    plan, own, held, chip_sums, *sums, sems = refs
    copies = [
        pltpu.make_async_copy(amplitudes, own, sems.at[0]),
        pltpu.make_async_copy(integrals, held, sems.at[1]),
    ]
    for copy in copies:
        copy.start()
    make_plan(axis, amplitudes.shape[0], tasks, plan)
    for ref in [chip_sums, *sums]:
        ref[...] = jnp.zeros_like(ref)
    for copy in copies:
        copy.wait()
    for kind, source in ((OWN, own), (CHIP, chip)):
        for (start, size), total in zip(chunks, sums):
            accumulate(plan, 3 * kind + CROSS, source, start, held, total, 0, size)
        accumulate(plan, 3 * kind + CHIP, source, 0, held, chip_sums, 0, chip.shape[1])


def cross_kernel(plan, integrals, sums, halo, total, rim):
    accumulate(plan, 3 * CROSS + CROSS, halo, 0, integrals, total, 0, halo.shape[1])
    rim[...] = total[...].astype(rim.dtype)


def rims_kernel(chunks, chip_chunks, plan, integrals, sums, chip_sums, *refs):
    halos, (*chip_rims, total, chip_total, rim) = refs[: len(chunks)], refs[len(chunks) :]
    accumulate(plan, 3 * CROSS + CROSS, halos[-1], 0, integrals, total, 0, total.shape[1])
    rim[...] = total[...].astype(rim.dtype)
    for (start, size), halo in zip(chunks, halos):
        accumulate(plan, 3 * CROSS + CHIP, halo, 0, integrals, chip_total, start, size)
    for (start, size), chip_rim in zip(chip_chunks, chip_rims):
        chip_rim[...] = chip_total[:, pl.ds(start, size)].astype(chip_rim.dtype)


def own_kernel(plan, own, integrals, chip, total):
    total[...] = jnp.zeros_like(total)
    accumulate(plan, 3 * OWN + OWN, own, 0, integrals, total, 0, own.shape[1])
    accumulate(plan, 3 * CHIP + OWN, chip, 0, integrals, total, 0, own.shape[1])


def resident_kernel(chunks, plan, integrals, sums, *refs):
    *halos, total = refs
    for (start, size), halo in zip(chunks, halos):
        accumulate(plan, 3 * CROSS + OWN, halo, 0, integrals, total, start, size)


def add_rim(first, chunks, sums, rims, out, part, sems):
    begin, end = chunks[0][0], sum(chunks[-1])
    copies = []
    for j in range(HALO):
        for (start, size), rim in zip(chunks, rims):
            rows = pl.ds(start - begin, size)
            part[j, rows] = sums[first + j, pl.ds(start, size)] + rim[j].astype(jnp.float32)
        target = out.at[first + j, pl.ds(begin, end - begin)]
        copies.append(pltpu.make_async_copy(part.at[j], target, sems.at[j]))
        copies[-1].start()
    for copy in copies:
        copy.wait()


def far_kernel(axis, chip_chunks, sums, *refs):
    rims, (*_, out, part, sems) = refs[: len(chip_chunks)], refs[len(chip_chunks) :]
    add_rim(edges(axis, out.shape[0])[1], chip_chunks, sums, rims, out, part, sems)


def near_kernel(axis, chunk, sums, rim, *refs):
    *_, out, part, sems = refs
    add_rim(edges(axis, out.shape[0])[0], [chunk], sums, [rim], out, part, sems)


def on_device(amplitudes, integrals, tasks):
    tile_count, rows, width = amplitudes.shape
    task_count = integrals.shape[0]
    chunks = row_chunks(rows, SPLIT)
    chip_chunks = row_chunks(rows, CHIP_SPLIT)
    count = len(chunks)
    axis = "own"
    devices = lax.axis_size(axis)
    cross_pairs = [(i, i + 1) for i in range(1, devices - 1, 2)]
    cross_pairs += [(b, a) for a, b in cross_pairs]
    chip_pairs = [(i, i ^ 1) for i in range(devices)]
    f32, bf16, i32 = jnp.float32, amplitudes.dtype, jnp.int32

    def call(kernel, name, operands, in_specs, after=(), **kwargs):
        here = len(operands)

        def body(*refs):
            kernel(*refs[:here], *refs[here + len(after) :])

        return pl.pallas_call(
            body,
            in_specs=in_specs + [pl.BlockSpec(memory_space=pl.ANY)] * len(after),
            compiler_params=pltpu.CompilerParams(vmem_limit_bytes=VMEM_LIMIT),
            cost_estimate=pl.CostEstimate(flops=1, bytes_accessed=1, transcendentals=0),
            name=name,
            **kwargs,
        )(*operands, *after)

    def swap_cross(x):
        return in_vmem(lax.ppermute(x, axis, cross_pairs))

    def swap_chip(x):
        return in_vmem(lax.ppermute(x, axis, chip_pairs))

    amplitudes, integrals = in_hbm(amplitudes), in_hbm(integrals)
    picked = call(
        functools.partial(pick_kernel, axis, chunks),
        "pick",
        [amplitudes],
        [hbm()],
        out_shape=[jax.ShapeDtypeStruct((HALO, size, width), bf16) for _, size in chunks]
        + [jax.ShapeDtypeStruct((HALO, rows, width), bf16)],
        out_specs=[hbm()] * (count + 1),
        scratch_shapes=[pltpu.SemaphoreType.DMA((count + 1,))],
    )
    halos = [swap_cross(x) for x in picked[:count]]
    chip_halo = swap_chip(picked[count])

    edge_shape = pltpu.VMEM((HALO, rows, width), f32)
    plan, own, held, chip_sums, *cross_sums = call(
        functools.partial(first_kernel, axis, chunks),
        "rim_targets",
        [tasks.T, amplitudes, integrals, chip_halo],
        [smem(), hbm(), hbm(), vmem()],
        out_shape=[
            jax.ShapeDtypeStruct((LISTS, task_count + 1), i32),
            pltpu.VMEM(amplitudes.shape, bf16),
            pltpu.VMEM(integrals.shape, bf16),
            edge_shape,
        ]
        + [pltpu.VMEM((HALO, size, width), f32) for _, size in chunks],
        out_specs=[smem()] + [vmem()] * (count + 3),
        scratch_shapes=[pltpu.SemaphoreType.DMA((2,))],
    )
    own, held, chip_sums = in_vmem(own), in_vmem(held), in_vmem(chip_sums)

    rims = []
    after = ()
    for i in range(count - 1):
        size = chunks[i][1]
        _, rim = call(
            cross_kernel,
            "cross_rim",
            [plan, held, in_vmem(cross_sums[i]), halos[i]],
            [smem()] + [vmem()] * 3,
            after=after,
            out_shape=[
                pltpu.VMEM((HALO, size, width), f32),
                pltpu.VMEM((HALO, size, width), bf16),
            ],
            out_specs=[vmem()] * 2,
            input_output_aliases={2: 0},
        )
        rims.append(rim)
        after = [in_vmem(rim)]
    resident_shape = pltpu.VMEM((tile_count, rows, width), f32)
    resident = call(
        own_kernel,
        "own_targets",
        [plan, own, held, chip_halo],
        [smem()] + [vmem()] * 3,
        after=after,
        out_shape=resident_shape,
        out_specs=vmem(),
    )
    resident = in_vmem(resident)
    size = chunks[-1][1]
    *chip_rims, _, _, rim = call(
        functools.partial(rims_kernel, chunks, chip_chunks),
        "last_rims",
        [plan, held, in_vmem(cross_sums[-1]), chip_sums, *halos],
        [smem()] + [vmem()] * (3 + count),
        after=[resident],
        out_shape=[pltpu.VMEM((HALO, part, width), bf16) for _, part in chip_chunks]
        + [
            pltpu.VMEM((HALO, size, width), f32),
            edge_shape,
            pltpu.VMEM((HALO, size, width), bf16),
        ],
        out_specs=[vmem()] * (3 + len(chip_chunks)),
        input_output_aliases={2: len(chip_chunks), 3: len(chip_chunks) + 1},
    )
    rims.append(rim)
    from_chip = [swap_chip(x) for x in chip_rims]
    from_cross = [swap_cross(x) for x in rims]
    resident = call(
        functools.partial(resident_kernel, chunks),
        "cross_sources",
        [plan, held, resident, *halos],
        [smem()] + [vmem()] * (2 + count),
        after=[in_vmem(rim)],
        out_shape=resident_shape,
        out_specs=vmem(),
        input_output_aliases={2: 0},
    )
    resident = in_vmem(resident)

    def write(kernel, name, blocks, length, out=None):
        before = [] if out is None else [out]
        return call(
            kernel,
            name,
            [resident, *blocks, *before],
            [vmem()] * (1 + len(blocks)) + [hbm()] * len(before),
            out_shape=jax.ShapeDtypeStruct((tile_count, rows, width), f32),
            out_specs=hbm(),
            scratch_shapes=[
                pltpu.VMEM((HALO, length, width), f32),
                pltpu.SemaphoreType.DMA((HALO,)),
            ],
            input_output_aliases={1 + len(blocks): 0} if before else {},
        )

    def near(i, out=None):
        kernel = functools.partial(near_kernel, axis, chunks[i])
        return write(kernel, "residual_near", [from_cross[i]], chunks[i][1], out)

    out = near(0)
    out = write(functools.partial(far_kernel, axis, chip_chunks), "residual_far", from_chip, rows, out)
    for i in range(1, count):
        out = near(i, out)
    return out


def solution(mesh):
    return jax.shard_map(
        on_device,
        mesh=mesh,
        in_specs=(
            P(("parts", "own"), None, None),
            P(("parts", "own"), None, None),
            P(("parts", "own"), None),
        ),
        out_specs=P(("parts", "own"), None, None),
        check_vma=False,
    )
```

```python
import functools

import jax
import jax.numpy as jnp
from jax import lax
from jax.experimental import pallas as pl
from jax.experimental.pallas import tpu as pltpu
from jax.sharding import PartitionSpec as P

HALO = 2
SPLIT = (512, 512)
CHIP_SPLIT = (384, 384, 256)
VMEM_LIMIT = 24 * 1024 * 1024

OWN, CHIP, CROSS = 0, 1, 2
LISTS = 9


def row_chunks(rows, split):
    total = sum(split)
    sizes = [rows * part // total for part in split]
    starts = [sum(sizes[:i]) for i in range(len(sizes))]
    return list(zip(starts, sizes))


def vmem():
    return pl.BlockSpec(memory_space=pltpu.VMEM)


def smem():
    return pl.BlockSpec(memory_space=pltpu.SMEM)


def hbm():
    return pl.BlockSpec(memory_space=pltpu.HBM)


def in_vmem(x):
    return pltpu.with_memory_space_constraint(x, pltpu.VMEM)


def in_hbm(x):
    return pltpu.with_memory_space_constraint(x, pltpu.HBM)


def accumulate(plan, which, integrals, segments):
    count = plan[which, plan.shape[1] - 1]

    def some(first, width):
        entries = [plan[which, first + u] for u in range(width)]
        for source, begin, sums, offset, size in segments:
            for r in range(0, size, 256):
                block = min(256, size - r)
                products = [
                    jnp.dot(
                        source[(entry >> 4) & 15, pl.ds(begin + r, block)],
                        integrals[entry >> 8],
                        preferred_element_type=jnp.float32,
                    )
                    for entry in entries
                ]
                for entry, product in zip(entries, products):
                    sums[entry & 15, pl.ds(offset + r, block)] += product

    def pair(i, carry):
        some(2 * i, 2)
        return carry

    def single(i, carry):
        some(i, 1)
        return carry

    pairs = count // 2
    lax.fori_loop(0, pairs, pair, 0)
    lax.fori_loop(2 * pairs, count, single, 0)


def overlaps(sources, totals):
    out = []
    start = 0
    for source in sources:
        end = start + source.shape[1]
        first = 0
        for total in totals:
            low, high = max(start, first), min(end, first + total.shape[1])
            if low < high:
                out.append((source, low - start, total, low - first, high - low))
            first += total.shape[1]
        start = end
    return out


def make_plan(axis, tile_count, tasks, plan):
    odd = lax.rem(lax.axis_index(axis), 2)
    first = lax.axis_index(axis) * tile_count
    last = plan.shape[1] - 1
    for which in range(LISTS):
        plan[which, last] = 0

    def place(tile):
        own = tile - first
        below = own < 0
        above = own >= tile_count
        crossing = jnp.logical_or(
            jnp.logical_and(below, odd == 0), jnp.logical_and(above, odd == 1)
        )
        slot = jnp.where(below, own + HALO, jnp.where(above, own - tile_count, own))
        kind = jnp.where(crossing, CROSS, jnp.where(jnp.logical_or(below, above), CHIP, OWN))
        return slot, kind

    def one(k, carry):
        src, src_kind = place(tasks[0, k])
        dst, dst_kind = place(tasks[1, k])
        which = 3 * src_kind + dst_kind
        count = plan[which, last]
        plan[which, count] = k * 256 + src * 16 + dst
        plan[which, last] = count + 1
        return carry

    lax.fori_loop(0, tasks.shape[1], one, 0)


def edges(axis, tile_count):
    odd = lax.rem(lax.axis_index(axis), 2)
    edge = tile_count - HALO
    return odd * edge, (1 - odd) * edge


def pick_kernel(axis, chunks, amplitudes, *refs):
    *picked, sems = refs
    near, _ = edges(axis, amplitudes.shape[0])
    copies = [
        pltpu.make_async_copy(
            amplitudes.at[pl.ds(near, HALO), pl.ds(start, size)], picked[i], sems.at[i]
        )
        for i, (start, size) in enumerate(chunks)
    ]
    for copy in copies:
        copy.start()
    for copy in copies:
        copy.wait()


def load_kernel(axis, chip_chunks, tasks, amplitudes, integrals, plan, own, held, *refs):
    *picked, sems = refs
    _, far = edges(axis, amplitudes.shape[0])
    copies = [
        pltpu.make_async_copy(amplitudes, own, sems.at[0]),
        pltpu.make_async_copy(integrals, held, sems.at[1]),
    ]
    for i, (start, size) in enumerate(chip_chunks):
        block = amplitudes.at[pl.ds(far, HALO), pl.ds(start, size)]
        copies.append(pltpu.make_async_copy(block, picked[i], sems.at[2 + i]))
    for copy in copies:
        copy.start()
    make_plan(axis, amplitudes.shape[0], tasks, plan)
    for copy in copies:
        copy.wait()


def own_rims_kernel(plan, own, integrals, chip_sums, *sums):
    for ref in [chip_sums, *sums]:
        ref[...] = jnp.zeros_like(ref)
    accumulate(plan, 3 * OWN + CROSS, integrals, overlaps([own], sums))
    accumulate(plan, 3 * OWN + CHIP, integrals, overlaps([own], [chip_sums]))


def chip_rims_kernel(parts, plan, integrals, *refs):
    chip, refs = refs[:parts], refs[parts:]
    chip_total, *totals = refs[len(refs) // 2 :]
    accumulate(plan, 3 * CHIP + CROSS, integrals, overlaps(chip, totals))
    accumulate(plan, 3 * CHIP + CHIP, integrals, overlaps(chip, [chip_total]))


def cross_kernel(plan, integrals, sums, halo, total, rim):
    accumulate(plan, 3 * CROSS + CROSS, integrals, overlaps([halo], [total]))
    rim[...] = total[...].astype(rim.dtype)


def rims_kernel(count, chip_chunks, plan, integrals, sums, chip_sums, *refs):
    halos, (*chip_rims, total, chip_total, rim) = refs[:count], refs[count:]
    accumulate(plan, 3 * CROSS + CROSS, integrals, overlaps([halos[-1]], [total]))
    rim[...] = total[...].astype(rim.dtype)
    accumulate(plan, 3 * CROSS + CHIP, integrals, overlaps(halos, [chip_total]))
    for (start, size), chip_rim in zip(chip_chunks, chip_rims):
        chip_rim[...] = chip_total[:, pl.ds(start, size)].astype(chip_rim.dtype)


def own_kernel(plan, own, integrals, total):
    total[...] = jnp.zeros_like(total)
    accumulate(plan, 3 * OWN + OWN, integrals, overlaps([own], [total]))


def resident_kernel(parts, plan, integrals, sums, *refs):
    *halos, total = refs
    accumulate(plan, 3 * CHIP + OWN, integrals, overlaps(halos[:parts], [total]))
    accumulate(plan, 3 * CROSS + OWN, integrals, overlaps(halos[parts:], [total]))


def add_rim(first, chunks, sums, rims, out, part, sems):
    begin, end = chunks[0][0], sum(chunks[-1])
    copies = []
    for j in range(HALO):
        for (start, size), rim in zip(chunks, rims):
            rows = pl.ds(start - begin, size)
            part[j, rows] = sums[first + j, pl.ds(start, size)] + rim[j].astype(jnp.float32)
        target = out.at[first + j, pl.ds(begin, end - begin)]
        copies.append(pltpu.make_async_copy(part.at[j], target, sems.at[j]))
        copies[-1].start()
    for copy in copies:
        copy.wait()


def far_kernel(axis, chip_chunks, sums, *refs):
    rims, (*_, out, part, sems) = refs[: len(chip_chunks)], refs[len(chip_chunks) :]
    add_rim(edges(axis, out.shape[0])[1], chip_chunks, sums, rims, out, part, sems)


def near_kernel(axis, chunk, sums, rim, *refs):
    *_, out, part, sems = refs
    add_rim(edges(axis, out.shape[0])[0], [chunk], sums, [rim], out, part, sems)


def on_device(amplitudes, integrals, tasks):
    tile_count, rows, width = amplitudes.shape
    task_count = integrals.shape[0]
    chunks = row_chunks(rows, SPLIT)
    chip_chunks = row_chunks(rows, CHIP_SPLIT)
    count = len(chunks)
    axis = "own"
    devices = lax.axis_size(axis)
    cross_pairs = [(i, i + 1) for i in range(1, devices - 1, 2)]
    cross_pairs += [(b, a) for a, b in cross_pairs]
    chip_pairs = [(i, i ^ 1) for i in range(devices)]
    f32, bf16, i32 = jnp.float32, amplitudes.dtype, jnp.int32

    def call(kernel, name, operands, in_specs, after=(), **kwargs):
        here = len(operands)

        def body(*refs):
            kernel(*refs[:here], *refs[here + len(after) :])

        return pl.pallas_call(
            body,
            in_specs=in_specs + [pl.BlockSpec(memory_space=pl.ANY)] * len(after),
            compiler_params=pltpu.CompilerParams(vmem_limit_bytes=VMEM_LIMIT),
            cost_estimate=pl.CostEstimate(flops=1, bytes_accessed=1, transcendentals=0),
            name=name,
            **kwargs,
        )(*operands, *after)

    def swap_cross(x):
        return in_vmem(lax.ppermute(x, axis, cross_pairs))

    def swap_chip(x):
        return in_vmem(lax.ppermute(x, axis, chip_pairs))

    amplitudes, integrals = in_hbm(amplitudes), in_hbm(integrals)
    picked = call(
        functools.partial(pick_kernel, axis, chunks),
        "pick",
        [amplitudes],
        [hbm()],
        out_shape=[jax.ShapeDtypeStruct((HALO, size, width), bf16) for _, size in chunks],
        out_specs=[hbm()] * count,
        scratch_shapes=[pltpu.SemaphoreType.DMA((count,))],
    )
    halos = [swap_cross(x) for x in picked]

    parts = len(chip_chunks)
    plan, own, held, *chip_picked = call(
        functools.partial(load_kernel, axis, chip_chunks),
        "load",
        [tasks.T, amplitudes, integrals],
        [smem(), hbm(), hbm()],
        after=picked,
        out_shape=[
            jax.ShapeDtypeStruct((LISTS, task_count + 1), i32),
            pltpu.VMEM(amplitudes.shape, bf16),
            pltpu.VMEM(integrals.shape, bf16),
        ]
        + [pltpu.VMEM((HALO, size, width), bf16) for _, size in chip_chunks],
        out_specs=[smem()] + [vmem()] * (2 + parts),
        scratch_shapes=[pltpu.SemaphoreType.DMA((2 + parts,))],
    )
    own, held = in_vmem(own), in_vmem(held)
    chip_halos = [swap_chip(x) for x in chip_picked]

    edge_shape = pltpu.VMEM((HALO, rows, width), f32)
    sums_shapes = [edge_shape] + [pltpu.VMEM((HALO, size, width), f32) for _, size in chunks]
    sums = call(
        own_rims_kernel,
        "own_rims",
        [plan, own, held],
        [smem()] + [vmem()] * 2,
        after=[in_vmem(x) for x in chip_picked],
        out_shape=sums_shapes,
        out_specs=[vmem()] * (count + 1),
    )
    chip_sums, *cross_sums = call(
        functools.partial(chip_rims_kernel, parts),
        "chip_rims",
        [plan, held, *chip_halos, *[in_vmem(x) for x in sums]],
        [smem()] + [vmem()] * (count + 2 + parts),
        out_shape=sums_shapes,
        out_specs=[vmem()] * (count + 1),
        input_output_aliases={2 + parts + i: i for i in range(count + 1)},
    )
    chip_sums = in_vmem(chip_sums)

    rims = []
    after = ()
    for i in range(count - 1):
        size = chunks[i][1]
        _, rim = call(
            cross_kernel,
            "cross_rim",
            [plan, held, in_vmem(cross_sums[i]), halos[i]],
            [smem()] + [vmem()] * 3,
            after=after,
            out_shape=[
                pltpu.VMEM((HALO, size, width), f32),
                pltpu.VMEM((HALO, size, width), bf16),
            ],
            out_specs=[vmem()] * 2,
            input_output_aliases={2: 0},
        )
        rims.append(rim)
        after = [in_vmem(rim)]
    resident_shape = pltpu.VMEM((tile_count, rows, width), f32)
    resident = call(
        own_kernel,
        "own_targets",
        [plan, own, held],
        [smem()] + [vmem()] * 2,
        after=after,
        out_shape=resident_shape,
        out_specs=vmem(),
    )
    resident = in_vmem(resident)
    size = chunks[-1][1]
    *chip_rims, _, _, rim = call(
        functools.partial(rims_kernel, count, chip_chunks),
        "last_rims",
        [plan, held, in_vmem(cross_sums[-1]), chip_sums, *halos],
        [smem()] + [vmem()] * (3 + count),
        after=[resident],
        out_shape=[pltpu.VMEM((HALO, part, width), bf16) for _, part in chip_chunks]
        + [
            pltpu.VMEM((HALO, size, width), f32),
            edge_shape,
            pltpu.VMEM((HALO, size, width), bf16),
        ],
        out_specs=[vmem()] * (3 + len(chip_chunks)),
        input_output_aliases={2: len(chip_chunks), 3: len(chip_chunks) + 1},
    )
    rims.append(rim)
    from_chip = [swap_chip(x) for x in chip_rims]
    from_cross = [swap_cross(x) for x in rims]
    resident = call(
        functools.partial(resident_kernel, parts),
        "halo_sources",
        [plan, held, resident, *chip_halos, *halos],
        [smem()] + [vmem()] * (2 + parts + count),
        after=[in_vmem(rim)],
        out_shape=resident_shape,
        out_specs=vmem(),
        input_output_aliases={2: 0},
    )
    resident = in_vmem(resident)

    def write(kernel, name, blocks, length, out=None):
        before = [] if out is None else [out]
        return call(
            kernel,
            name,
            [resident, *blocks, *before],
            [vmem()] * (1 + len(blocks)) + [hbm()] * len(before),
            out_shape=jax.ShapeDtypeStruct((tile_count, rows, width), f32),
            out_specs=hbm(),
            scratch_shapes=[
                pltpu.VMEM((HALO, length, width), f32),
                pltpu.SemaphoreType.DMA((HALO,)),
            ],
            input_output_aliases={1 + len(blocks): 0} if before else {},
        )

    def near(i, out=None):
        kernel = functools.partial(near_kernel, axis, chunks[i])
        return write(kernel, "residual_near", [from_cross[i]], chunks[i][1], out)

    out = near(0)
    out = write(functools.partial(far_kernel, axis, chip_chunks), "residual_far", from_chip, rows, out)
    for i in range(1, count):
        out = near(i, out)
    return out


def solution(mesh):
    return jax.shard_map(
        on_device,
        mesh=mesh,
        in_specs=(
            P(("parts", "own"), None, None),
            P(("parts", "own"), None, None),
            P(("parts", "own"), None),
        ),
        out_specs=P(("parts", "own"), None, None),
        check_vma=False,
    )
```

```python
import functools

import jax
import jax.numpy as jnp
from jax import lax
from jax.experimental import pallas as pl
from jax.experimental.pallas import tpu as pltpu
from jax.sharding import PartitionSpec as P

HALO = 2
SPLIT = (512, 512)
CHIP_SPLIT = (384, 384, 256)
VMEM_LIMIT = 24 * 1024 * 1024

OWN, CHIP, CROSS = 0, 1, 2
LISTS = 9
GROUPS = 3


def row_chunks(rows, split):
    total = sum(split)
    sizes = [rows * part // total for part in split]
    starts = [sum(sizes[:i]) for i in range(len(sizes))]
    return list(zip(starts, sizes))


def vmem():
    return pl.BlockSpec(memory_space=pltpu.VMEM)


def smem():
    return pl.BlockSpec(memory_space=pltpu.SMEM)


def hbm():
    return pl.BlockSpec(memory_space=pltpu.HBM)


def in_vmem(x):
    return pltpu.with_memory_space_constraint(x, pltpu.VMEM)


def in_hbm(x):
    return pltpu.with_memory_space_constraint(x, pltpu.HBM)


def accumulate(plan, which, integrals, segments, begin=0, end=None):
    end = plan[which, plan.shape[1] - 1] if end is None else end

    def some(first, width):
        entries = [plan[which, first + u] for u in range(width)]
        for source, low, sums, offset, size in segments:
            for r in range(0, size, 256):
                block = min(256, size - r)
                products = [
                    jnp.dot(
                        source[(entry >> 4) & 15, pl.ds(low + r, block)],
                        integrals[entry >> 8],
                        preferred_element_type=jnp.float32,
                    )
                    for entry in entries
                ]
                for entry, product in zip(entries, products):
                    sums[entry & 15, pl.ds(offset + r, block)] += product

    def pair(i, carry):
        some(begin + 2 * i, 2)
        return carry

    def single(i, carry):
        some(i, 1)
        return carry

    pairs = (end - begin) // 2
    lax.fori_loop(0, pairs, pair, 0)
    lax.fori_loop(begin + 2 * pairs, end, single, 0)


def overlaps(sources, totals):
    out = []
    start = 0
    for source in sources:
        end = start + source.shape[1]
        first = 0
        for total in totals:
            low, high = max(start, first), min(end, first + total.shape[1])
            if low < high:
                out.append((source, low - start, total, low - first, high - low))
            first += total.shape[1]
        start = end
    return out


def make_plan(axis, tile_count, tasks, plan):
    odd = lax.rem(lax.axis_index(axis), 2)
    first = lax.axis_index(axis) * tile_count
    last = plan.shape[1] - 1
    for which in range(LISTS):
        plan[which, last] = 0

    def place(tile):
        own = tile - first
        below = own < 0
        above = own >= tile_count
        crossing = jnp.logical_or(
            jnp.logical_and(below, odd == 0), jnp.logical_and(above, odd == 1)
        )
        slot = jnp.where(below, own + HALO, jnp.where(above, own - tile_count, own))
        kind = jnp.where(crossing, CROSS, jnp.where(jnp.logical_or(below, above), CHIP, OWN))
        return slot, kind

    def one(k, carry):
        src, src_kind = place(tasks[0, k])
        dst, dst_kind = place(tasks[1, k])
        which = 3 * src_kind + dst_kind
        count = plan[which, last]
        plan[which, count] = k * 256 + src * 16 + dst
        plan[which, last] = count + 1
        return carry

    ends = []
    size = tasks.shape[1] // GROUPS
    for group in range(GROUPS):
        lax.fori_loop(group * size, (group + 1) * size, one, 0)
        ends.append([plan[3 * OWN + kind, last] for kind in (OWN, CHIP, CROSS)])
    return ends


def edges(axis, tile_count):
    odd = lax.rem(lax.axis_index(axis), 2)
    edge = tile_count - HALO
    return odd * edge, (1 - odd) * edge


def pick_kernel(axis, near_rows, far_rows, amplitudes, *refs):
    *picked, sems = refs
    near, far = edges(axis, amplitudes.shape[0])
    copies = []
    for first, some in ((near, near_rows), (far, far_rows)):
        for rows in some:
            i = len(copies)
            block = amplitudes.at[pl.ds(first, HALO), pl.ds(*rows)]
            copies.append(pltpu.make_async_copy(block, picked[i], sems.at[i]))
            copies[-1].start()
    for copy in copies:
        copy.wait()


def first_kernel(axis, tasks, amplitudes, integrals, plan, own, held, chip_sums, *refs):
    *sums, sems = refs
    size = integrals.shape[0] // GROUPS
    copies = [pltpu.make_async_copy(amplitudes, own, sems.at[GROUPS])]
    for group in range(GROUPS):
        tasks_in_it = pl.ds(group * size, size)
        copies.append(
            pltpu.make_async_copy(
                integrals.at[tasks_in_it], held.at[tasks_in_it], sems.at[group]
            )
        )
    for copy in copies:
        copy.start()
    ends = make_plan(axis, amplitudes.shape[0], tasks, plan)
    for ref in [chip_sums, *sums]:
        ref[...] = jnp.zeros_like(ref)
    copies[0].wait()
    begins = [0] * 3
    for copy, now in zip(copies[1:], ends):
        copy.wait()
        for kind, totals in ((CROSS, sums), (CHIP, [chip_sums])):
            segments = overlaps([own], totals)
            accumulate(plan, 3 * OWN + kind, held, segments, begins[kind], now[kind])
        begins = now


def chip_rims_kernel(parts, plan, integrals, *refs):
    chip, refs = refs[:parts], refs[parts:]
    chip_total, *totals = refs[len(refs) // 2 :]
    accumulate(plan, 3 * CHIP + CROSS, integrals, overlaps(chip, totals))
    accumulate(plan, 3 * CHIP + CHIP, integrals, overlaps(chip, [chip_total]))


def cross_kernel(plan, integrals, sums, halo, total, rim):
    accumulate(plan, 3 * CROSS + CROSS, integrals, overlaps([halo], [total]))
    rim[...] = total[...].astype(rim.dtype)


def rims_kernel(count, chip_chunks, plan, integrals, sums, chip_sums, *refs):
    halos, (*chip_rims, total, chip_total, rim) = refs[:count], refs[count:]
    accumulate(plan, 3 * CROSS + CROSS, integrals, overlaps([halos[-1]], [total]))
    rim[...] = total[...].astype(rim.dtype)
    accumulate(plan, 3 * CROSS + CHIP, integrals, overlaps(halos, [chip_total]))
    for (start, size), chip_rim in zip(chip_chunks, chip_rims):
        chip_rim[...] = chip_total[:, pl.ds(start, size)].astype(chip_rim.dtype)


def own_kernel(plan, own, integrals, *refs):
    *chip, total = refs
    total[...] = jnp.zeros_like(total)
    accumulate(plan, 3 * OWN + OWN, integrals, overlaps([own], [total]))
    accumulate(plan, 3 * CHIP + OWN, integrals, overlaps(chip, [total]))


def resident_kernel(plan, integrals, sums, *refs):
    *halos, total = refs
    accumulate(plan, 3 * CROSS + OWN, integrals, overlaps(halos, [total]))


def add_rim(places, sums, out, sems):
    copies = []
    for first, rims, begin, part, sem in places:
        row = 0
        for rim in rims:
            size = rim.shape[1]
            here, there = pl.ds(row, size), pl.ds(begin + row, size)
            for j in range(HALO):
                part[j, here] = sums[first + j, there] + rim[j].astype(jnp.float32)
            copies.append(
                pltpu.make_async_copy(
                    part.at[:, here], out.at[pl.ds(first, HALO), there], sems.at[sem]
                )
            )
            copies[-1].start()
            sem += 1
            row += size
    for copy in copies:
        copy.wait()


def rest_kernel(axis, parts, sums, *refs):
    rims, (out, part, sems) = refs[:-3], refs[-3:]
    near, far = edges(axis, out.shape[0])
    places = [
        (far, rims[:parts], 0, part.at[pl.ds(0, HALO)], 0),
        (near, rims[parts:], 0, part.at[pl.ds(HALO, HALO)], parts),
    ]
    add_rim(places, sums, out, sems)


def last_kernel(axis, begin, sums, rim, before, out, part, sems):
    near, _ = edges(axis, out.shape[0])
    add_rim([(near, [rim], begin, part, 0)], sums, out, sems)


def on_device(amplitudes, integrals, tasks):
    tile_count, rows, width = amplitudes.shape
    task_count = integrals.shape[0]
    chunks = row_chunks(rows, SPLIT)
    chip_chunks = row_chunks(rows, CHIP_SPLIT)
    count = len(chunks)
    axis = "own"
    devices = lax.axis_size(axis)
    cross_pairs = [(i, i + 1) for i in range(1, devices - 1, 2)]
    cross_pairs += [(b, a) for a, b in cross_pairs]
    chip_pairs = [(i, i ^ 1) for i in range(devices)]
    f32, bf16, i32 = jnp.float32, amplitudes.dtype, jnp.int32

    def call(kernel, name, operands, in_specs, after=(), **kwargs):
        here = len(operands)

        def body(*refs):
            kernel(*refs[:here], *refs[here + len(after) :])

        return pl.pallas_call(
            body,
            in_specs=in_specs + [pl.BlockSpec(memory_space=pl.ANY)] * len(after),
            compiler_params=pltpu.CompilerParams(vmem_limit_bytes=VMEM_LIMIT),
            cost_estimate=pl.CostEstimate(flops=1, bytes_accessed=1, transcendentals=0),
            name=name,
            **kwargs,
        )(*operands, *after)

    def swap_cross(x):
        return in_vmem(lax.ppermute(x, axis, cross_pairs))

    def swap_chip(x):
        return in_vmem(lax.ppermute(x, axis, chip_pairs))

    amplitudes, integrals = in_hbm(amplitudes), in_hbm(integrals)
    def pick(near_rows, far_rows, after=()):
        sizes = [size for _, size in near_rows + far_rows]
        return call(
            functools.partial(pick_kernel, axis, near_rows, far_rows),
            "pick",
            [amplitudes],
            [hbm()],
            after=after,
            out_shape=[jax.ShapeDtypeStruct((HALO, size, width), bf16) for size in sizes],
            out_specs=[hbm()] * len(sizes),
            scratch_shapes=[pltpu.SemaphoreType.DMA((len(sizes),))],
        )

    parts = len(chip_chunks)
    head = pick(chunks[:1], [])
    rest = pick(chunks[1:], chip_chunks, after=head)
    halos = [swap_cross(x) for x in head + rest[: count - 1]]
    chip_halos = [swap_chip(x) for x in rest[count - 1 :]]

    edge_shape = pltpu.VMEM((HALO, rows, width), f32)
    sums_shapes = [edge_shape] + [pltpu.VMEM((HALO, size, width), f32) for _, size in chunks]
    plan, own, held, *sums = call(
        functools.partial(first_kernel, axis),
        "own_rims",
        [tasks.T, amplitudes, integrals],
        [smem(), hbm(), hbm()],
        after=rest,
        out_shape=[
            jax.ShapeDtypeStruct((LISTS, task_count + 1), i32),
            pltpu.VMEM(amplitudes.shape, bf16),
            pltpu.VMEM(integrals.shape, bf16),
        ]
        + sums_shapes,
        out_specs=[smem()] + [vmem()] * (3 + count),
        scratch_shapes=[pltpu.SemaphoreType.DMA((1 + GROUPS,))],
    )
    own, held = in_vmem(own), in_vmem(held)
    chip_sums, *cross_sums = call(
        functools.partial(chip_rims_kernel, parts),
        "chip_rims",
        [plan, held, *chip_halos, *[in_vmem(x) for x in sums]],
        [smem()] + [vmem()] * (count + 2 + parts),
        out_shape=sums_shapes,
        out_specs=[vmem()] * (count + 1),
        input_output_aliases={2 + parts + i: i for i in range(count + 1)},
    )
    chip_sums = in_vmem(chip_sums)

    rims = []
    after = ()
    for i in range(count - 1):
        size = chunks[i][1]
        _, rim = call(
            cross_kernel,
            "cross_rim",
            [plan, held, in_vmem(cross_sums[i]), halos[i]],
            [smem()] + [vmem()] * 3,
            after=after,
            out_shape=[
                pltpu.VMEM((HALO, size, width), f32),
                pltpu.VMEM((HALO, size, width), bf16),
            ],
            out_specs=[vmem()] * 2,
            input_output_aliases={2: 0},
        )
        rims.append(rim)
        after = [in_vmem(rim)]
    resident_shape = pltpu.VMEM((tile_count, rows, width), f32)
    resident = call(
        own_kernel,
        "own_targets",
        [plan, own, held, *chip_halos],
        [smem()] + [vmem()] * (2 + parts),
        after=after,
        out_shape=resident_shape,
        out_specs=vmem(),
    )
    resident = in_vmem(resident)
    size = chunks[-1][1]
    *chip_rims, _, _, rim = call(
        functools.partial(rims_kernel, count, chip_chunks),
        "last_rims",
        [plan, held, in_vmem(cross_sums[-1]), chip_sums, *halos],
        [smem()] + [vmem()] * (3 + count),
        after=[resident],
        out_shape=[pltpu.VMEM((HALO, part, width), bf16) for _, part in chip_chunks]
        + [
            pltpu.VMEM((HALO, size, width), f32),
            edge_shape,
            pltpu.VMEM((HALO, size, width), bf16),
        ],
        out_specs=[vmem()] * (3 + len(chip_chunks)),
        input_output_aliases={2: len(chip_chunks), 3: len(chip_chunks) + 1},
    )
    rims.append(rim)
    from_chip = [swap_chip(x) for x in chip_rims]
    from_cross = [swap_cross(x) for x in rims]
    resident = call(
        resident_kernel,
        "cross_sources",
        [plan, held, resident, *halos],
        [smem()] + [vmem()] * (2 + count),
        after=[in_vmem(rim)],
        out_shape=resident_shape,
        out_specs=vmem(),
        input_output_aliases={2: 0},
    )
    resident = in_vmem(resident)

    shape = jax.ShapeDtypeStruct((tile_count, rows, width), f32)
    blocks = from_chip + from_cross[:-1]
    out = call(
        functools.partial(rest_kernel, axis, parts),
        "residual",
        [resident, *blocks],
        [vmem()] * (1 + len(blocks)),
        out_shape=shape,
        out_specs=hbm(),
        scratch_shapes=[
            pltpu.VMEM((2 * HALO, rows, width), f32),
            pltpu.SemaphoreType.DMA((len(blocks),)),
        ],
    )
    begin, size = chunks[-1]
    return call(
        functools.partial(last_kernel, axis, begin),
        "residual_last",
        [resident, from_cross[-1], out],
        [vmem()] * 2 + [hbm()],
        out_shape=shape,
        out_specs=hbm(),
        scratch_shapes=[
            pltpu.VMEM((HALO, size, width), f32),
            pltpu.SemaphoreType.DMA((1,)),
        ],
        input_output_aliases={2: 0},
    )


def solution(mesh):
    return jax.shard_map(
        on_device,
        mesh=mesh,
        in_specs=(
            P(("parts", "own"), None, None),
            P(("parts", "own"), None, None),
            P(("parts", "own"), None),
        ),
        out_specs=P(("parts", "own"), None, None),
        check_vma=False,
    )
```

```python
import functools

import jax
import jax.numpy as jnp
from jax import lax
from jax.experimental import pallas as pl
from jax.experimental.pallas import tpu as pltpu
from jax.sharding import PartitionSpec as P

HALO = 2
SPLIT = (544, 480)
CHIP_SPLIT = (384, 384, 256)
VMEM_LIMIT = 24 * 1024 * 1024

OWN, CHIP, CROSS = 0, 1, 2
LISTS = 9
GROUPS = 3


def row_chunks(rows, split):
    total = sum(split)
    sizes = [rows * part // total for part in split]
    starts = [sum(sizes[:i]) for i in range(len(sizes))]
    return list(zip(starts, sizes))


def vmem():
    return pl.BlockSpec(memory_space=pltpu.VMEM)


def smem():
    return pl.BlockSpec(memory_space=pltpu.SMEM)


def hbm():
    return pl.BlockSpec(memory_space=pltpu.HBM)


def in_vmem(x):
    return pltpu.with_memory_space_constraint(x, pltpu.VMEM)


def in_hbm(x):
    return pltpu.with_memory_space_constraint(x, pltpu.HBM)


def accumulate(plan, which, integrals, segments, begin=0, end=None):
    end = plan[which, plan.shape[1] - 1] if end is None else end

    def some(first, width):
        entries = [plan[which, first + u] for u in range(width)]
        for source, low, sums, offset, size in segments:
            for r in range(0, size, 256):
                block = min(256, size - r)
                products = [
                    jnp.dot(
                        source[(entry >> 4) & 15, pl.ds(low + r, block)],
                        integrals[entry >> 8],
                        preferred_element_type=jnp.float32,
                    )
                    for entry in entries
                ]
                for entry, product in zip(entries, products):
                    sums[entry & 15, pl.ds(offset + r, block)] += product

    def pair(i, carry):
        some(begin + 2 * i, 2)
        return carry

    def single(i, carry):
        some(i, 1)
        return carry

    pairs = (end - begin) // 2
    lax.fori_loop(0, pairs, pair, 0)
    lax.fori_loop(begin + 2 * pairs, end, single, 0)


def overlaps(sources, totals):
    out = []
    start = 0
    for source in sources:
        end = start + source.shape[1]
        first = 0
        for total in totals:
            low, high = max(start, first), min(end, first + total.shape[1])
            if low < high:
                out.append((source, low - start, total, low - first, high - low))
            first += total.shape[1]
        start = end
    return out


def make_plan(axis, tile_count, tasks, plan):
    odd = lax.rem(lax.axis_index(axis), 2)
    first = lax.axis_index(axis) * tile_count
    last = plan.shape[1] - 1
    for which in range(LISTS):
        plan[which, last] = 0

    def place(tile):
        own = tile - first
        below = own < 0
        above = own >= tile_count
        crossing = jnp.logical_or(
            jnp.logical_and(below, odd == 0), jnp.logical_and(above, odd == 1)
        )
        slot = jnp.where(below, own + HALO, jnp.where(above, own - tile_count, own))
        kind = jnp.where(crossing, CROSS, jnp.where(jnp.logical_or(below, above), CHIP, OWN))
        return slot, kind

    def one(k, carry):
        src, src_kind = place(tasks[0, k])
        dst, dst_kind = place(tasks[1, k])
        which = 3 * src_kind + dst_kind
        count = plan[which, last]
        plan[which, count] = k * 256 + src * 16 + dst
        plan[which, last] = count + 1
        return carry

    ends = []
    size = tasks.shape[1] // GROUPS
    for group in range(GROUPS):
        lax.fori_loop(group * size, (group + 1) * size, one, 0)
        ends.append([plan[3 * OWN + kind, last] for kind in (OWN, CHIP, CROSS)])
    return ends


def edges(axis, tile_count):
    odd = lax.rem(lax.axis_index(axis), 2)
    edge = tile_count - HALO
    return odd * edge, (1 - odd) * edge


def pick_kernel(axis, near_rows, far_rows, amplitudes, *refs):
    *picked, sems = refs
    near, far = edges(axis, amplitudes.shape[0])
    copies = []
    for first, some in ((near, near_rows), (far, far_rows)):
        for rows in some:
            i = len(copies)
            block = amplitudes.at[pl.ds(first, HALO), pl.ds(*rows)]
            copies.append(pltpu.make_async_copy(block, picked[i], sems.at[i]))
            copies[-1].start()
    for copy in copies:
        copy.wait()


def first_kernel(axis, tasks, amplitudes, integrals, plan, own, held, chip_sums, *refs):
    *sums, sems = refs
    size = integrals.shape[0] // GROUPS
    copies = [pltpu.make_async_copy(amplitudes, own, sems.at[GROUPS])]
    for group in range(GROUPS):
        tasks_in_it = pl.ds(group * size, size)
        copies.append(
            pltpu.make_async_copy(
                integrals.at[tasks_in_it], held.at[tasks_in_it], sems.at[group]
            )
        )
    for copy in copies:
        copy.start()
    ends = make_plan(axis, amplitudes.shape[0], tasks, plan)
    for ref in [chip_sums, *sums]:
        ref[...] = jnp.zeros_like(ref)
    copies[0].wait()
    begins = [0] * 3
    for copy, now in zip(copies[1:], ends):
        copy.wait()
        for kind, totals in ((CROSS, sums), (CHIP, [chip_sums])):
            segments = overlaps([own], totals)
            accumulate(plan, 3 * OWN + kind, held, segments, begins[kind], now[kind])
        begins = now


def chip_rims_kernel(parts, plan, integrals, *refs):
    chip, refs = refs[:parts], refs[parts:]
    chip_total, *totals = refs[len(refs) // 2 :]
    accumulate(plan, 3 * CHIP + CROSS, integrals, overlaps(chip, totals))
    accumulate(plan, 3 * CHIP + CHIP, integrals, overlaps(chip, [chip_total]))


def cross_kernel(plan, integrals, sums, halo, total, rim):
    accumulate(plan, 3 * CROSS + CROSS, integrals, overlaps([halo], [total]))
    rim[...] = total[...].astype(rim.dtype)


def rims_kernel(count, chip_chunks, plan, integrals, sums, chip_sums, *refs):
    halos, (*chip_rims, total, chip_total, rim) = refs[:count], refs[count:]
    accumulate(plan, 3 * CROSS + CROSS, integrals, overlaps([halos[-1]], [total]))
    rim[...] = total[...].astype(rim.dtype)
    accumulate(plan, 3 * CROSS + CHIP, integrals, overlaps(halos, [chip_total]))
    for (start, size), chip_rim in zip(chip_chunks, chip_rims):
        chip_rim[...] = chip_total[:, pl.ds(start, size)].astype(chip_rim.dtype)


def own_kernel(plan, own, integrals, *refs):
    *chip, total = refs
    total[...] = jnp.zeros_like(total)
    accumulate(plan, 3 * OWN + OWN, integrals, overlaps([own], [total]))
    accumulate(plan, 3 * CHIP + OWN, integrals, overlaps(chip, [total]))


def resident_kernel(plan, integrals, sums, *refs):
    *halos, total = refs
    accumulate(plan, 3 * CROSS + OWN, integrals, overlaps(halos, [total]))


def add_rim(places, sums, out, sems):
    copies = []
    for first, rims, begin, part, sem in places:
        row = 0
        for rim in rims:
            size = rim.shape[1]
            here, there = pl.ds(row, size), pl.ds(begin + row, size)
            for j in range(HALO):
                part[j, here] = sums[first + j, there] + rim[j].astype(jnp.float32)
            copies.append(
                pltpu.make_async_copy(
                    part.at[:, here], out.at[pl.ds(first, HALO), there], sems.at[sem]
                )
            )
            copies[-1].start()
            sem += 1
            row += size
    for copy in copies:
        copy.wait()


def rest_kernel(axis, parts, sums, *refs):
    rims, (out, part, sems) = refs[:-3], refs[-3:]
    near, far = edges(axis, out.shape[0])
    places = [
        (far, rims[:parts], 0, part.at[pl.ds(0, HALO)], 0),
        (near, rims[parts:], 0, part.at[pl.ds(HALO, HALO)], parts),
    ]
    add_rim(places, sums, out, sems)


def last_kernel(axis, begin, sums, rim, before, out, part, sems):
    near, _ = edges(axis, out.shape[0])
    add_rim([(near, [rim], begin, part, 0)], sums, out, sems)


def on_device(amplitudes, integrals, tasks):
    tile_count, rows, width = amplitudes.shape
    task_count = integrals.shape[0]
    chunks = row_chunks(rows, SPLIT)
    chip_chunks = row_chunks(rows, CHIP_SPLIT)
    count = len(chunks)
    axis = "own"
    devices = lax.axis_size(axis)
    cross_pairs = [(i, i + 1) for i in range(1, devices - 1, 2)]
    cross_pairs += [(b, a) for a, b in cross_pairs]
    chip_pairs = [(i, i ^ 1) for i in range(devices)]
    f32, bf16, i32 = jnp.float32, amplitudes.dtype, jnp.int32

    def call(kernel, name, operands, in_specs, after=(), **kwargs):
        here = len(operands)

        def body(*refs):
            kernel(*refs[:here], *refs[here + len(after) :])

        return pl.pallas_call(
            body,
            in_specs=in_specs + [pl.BlockSpec(memory_space=pl.ANY)] * len(after),
            compiler_params=pltpu.CompilerParams(vmem_limit_bytes=VMEM_LIMIT),
            cost_estimate=pl.CostEstimate(flops=1, bytes_accessed=1, transcendentals=0),
            name=name,
            **kwargs,
        )(*operands, *after)

    def swap_cross(x):
        return in_vmem(lax.ppermute(x, axis, cross_pairs))

    def swap_chip(x):
        return in_vmem(lax.ppermute(x, axis, chip_pairs))

    amplitudes, integrals = in_hbm(amplitudes), in_hbm(integrals)
    def pick(near_rows, far_rows, after=()):
        sizes = [size for _, size in near_rows + far_rows]
        return call(
            functools.partial(pick_kernel, axis, near_rows, far_rows),
            "pick",
            [amplitudes],
            [hbm()],
            after=after,
            out_shape=[jax.ShapeDtypeStruct((HALO, size, width), bf16) for size in sizes],
            out_specs=[hbm()] * len(sizes),
            scratch_shapes=[pltpu.SemaphoreType.DMA((len(sizes),))],
        )

    parts = len(chip_chunks)
    head = pick(chunks[:1], [])
    rest = pick(chunks[1:], chip_chunks, after=head)
    halos = [swap_cross(x) for x in head + rest[: count - 1]]
    chip_halos = [swap_chip(x) for x in rest[count - 1 :]]

    edge_shape = pltpu.VMEM((HALO, rows, width), f32)
    sums_shapes = [edge_shape] + [pltpu.VMEM((HALO, size, width), f32) for _, size in chunks]
    plan, own, held, *sums = call(
        functools.partial(first_kernel, axis),
        "own_rims",
        [tasks.T, amplitudes, integrals],
        [smem(), hbm(), hbm()],
        after=rest,
        out_shape=[
            jax.ShapeDtypeStruct((LISTS, task_count + 1), i32),
            pltpu.VMEM(amplitudes.shape, bf16),
            pltpu.VMEM(integrals.shape, bf16),
        ]
        + sums_shapes,
        out_specs=[smem()] + [vmem()] * (3 + count),
        scratch_shapes=[pltpu.SemaphoreType.DMA((1 + GROUPS,))],
    )
    own, held = in_vmem(own), in_vmem(held)
    chip_sums, *cross_sums = call(
        functools.partial(chip_rims_kernel, parts),
        "chip_rims",
        [plan, held, *chip_halos, *[in_vmem(x) for x in sums]],
        [smem()] + [vmem()] * (count + 2 + parts),
        out_shape=sums_shapes,
        out_specs=[vmem()] * (count + 1),
        input_output_aliases={2 + parts + i: i for i in range(count + 1)},
    )
    chip_sums = in_vmem(chip_sums)

    rims = []
    after = ()
    for i in range(count - 1):
        size = chunks[i][1]
        _, rim = call(
            cross_kernel,
            "cross_rim",
            [plan, held, in_vmem(cross_sums[i]), halos[i]],
            [smem()] + [vmem()] * 3,
            after=after,
            out_shape=[
                pltpu.VMEM((HALO, size, width), f32),
                pltpu.VMEM((HALO, size, width), bf16),
            ],
            out_specs=[vmem()] * 2,
            input_output_aliases={2: 0},
        )
        rims.append(rim)
        after = [in_vmem(rim)]
    resident_shape = pltpu.VMEM((tile_count, rows, width), f32)
    resident = call(
        own_kernel,
        "own_targets",
        [plan, own, held, *chip_halos],
        [smem()] + [vmem()] * (2 + parts),
        after=after,
        out_shape=resident_shape,
        out_specs=vmem(),
    )
    resident = in_vmem(resident)
    size = chunks[-1][1]
    *chip_rims, _, _, rim = call(
        functools.partial(rims_kernel, count, chip_chunks),
        "last_rims",
        [plan, held, in_vmem(cross_sums[-1]), chip_sums, *halos],
        [smem()] + [vmem()] * (3 + count),
        after=[resident],
        out_shape=[pltpu.VMEM((HALO, part, width), bf16) for _, part in chip_chunks]
        + [
            pltpu.VMEM((HALO, size, width), f32),
            edge_shape,
            pltpu.VMEM((HALO, size, width), bf16),
        ],
        out_specs=[vmem()] * (3 + len(chip_chunks)),
        input_output_aliases={2: len(chip_chunks), 3: len(chip_chunks) + 1},
    )
    rims.append(rim)
    from_chip = [swap_chip(x) for x in chip_rims]
    from_cross = [swap_cross(x) for x in rims]
    resident = call(
        resident_kernel,
        "cross_sources",
        [plan, held, resident, *halos],
        [smem()] + [vmem()] * (2 + count),
        after=[in_vmem(rim)],
        out_shape=resident_shape,
        out_specs=vmem(),
        input_output_aliases={2: 0},
    )
    resident = in_vmem(resident)

    shape = jax.ShapeDtypeStruct((tile_count, rows, width), f32)
    blocks = from_chip + from_cross[:-1]
    out = call(
        functools.partial(rest_kernel, axis, parts),
        "residual",
        [resident, *blocks],
        [vmem()] * (1 + len(blocks)),
        out_shape=shape,
        out_specs=hbm(),
        scratch_shapes=[
            pltpu.VMEM((2 * HALO, rows, width), f32),
            pltpu.SemaphoreType.DMA((len(blocks),)),
        ],
    )
    begin, size = chunks[-1]
    return call(
        functools.partial(last_kernel, axis, begin),
        "residual_last",
        [resident, from_cross[-1], out],
        [vmem()] * 2 + [hbm()],
        out_shape=shape,
        out_specs=hbm(),
        scratch_shapes=[
            pltpu.VMEM((HALO, size, width), f32),
            pltpu.SemaphoreType.DMA((1,)),
        ],
        input_output_aliases={2: 0},
    )


def solution(mesh):
    return jax.shard_map(
        on_device,
        mesh=mesh,
        in_specs=(
            P(("parts", "own"), None, None),
            P(("parts", "own"), None, None),
            P(("parts", "own"), None),
        ),
        out_specs=P(("parts", "own"), None, None),
        check_vma=False,
    )
```

```python
import functools

import jax
import jax.numpy as jnp
from jax import lax
from jax.experimental import pallas as pl
from jax.experimental.pallas import tpu as pltpu
from jax.sharding import PartitionSpec as P

HALO = 2
SPLIT = (512, 512)
RIM_SPLIT = (512, 432, 80)
CHIP_RIM_SPLIT = (352, 336, 336)
CHIP_SPLIT = (384, 384, 256)
VMEM_LIMIT = 24 * 1024 * 1024

OWN, CHIP, CROSS = 0, 1, 2
LISTS = 9
GROUPS = 3


def row_chunks(rows, split):
    total = sum(split)
    sizes = [rows * part // total for part in split]
    starts = [sum(sizes[:i]) for i in range(len(sizes))]
    return list(zip(starts, sizes))


def vmem():
    return pl.BlockSpec(memory_space=pltpu.VMEM)


def smem():
    return pl.BlockSpec(memory_space=pltpu.SMEM)


def hbm():
    return pl.BlockSpec(memory_space=pltpu.HBM)


def in_vmem(x):
    return pltpu.with_memory_space_constraint(x, pltpu.VMEM)


def in_hbm(x):
    return pltpu.with_memory_space_constraint(x, pltpu.HBM)


def accumulate(plan, which, integrals, segments, begin=0, end=None):
    end = plan[which, plan.shape[1] - 1] if end is None else end

    def some(first, width):
        entries = [plan[which, first + u] for u in range(width)]
        for source, low, sums, offset, size in segments:
            for r in range(0, size, 256):
                block = min(256, size - r)
                products = [
                    jnp.dot(
                        source[(entry >> 4) & 15, pl.ds(low + r, block)],
                        integrals[entry >> 8],
                        preferred_element_type=jnp.float32,
                    )
                    for entry in entries
                ]
                for entry, product in zip(entries, products):
                    sums[entry & 15, pl.ds(offset + r, block)] += product

    def pair(i, carry):
        some(begin + 2 * i, 2)
        return carry

    def single(i, carry):
        some(i, 1)
        return carry

    pairs = (end - begin) // 2
    lax.fori_loop(0, pairs, pair, 0)
    lax.fori_loop(begin + 2 * pairs, end, single, 0)


def overlaps(sources, totals):
    out = []
    start = 0
    for source in sources:
        end = start + source.shape[1]
        first = 0
        for total in totals:
            low, high = max(start, first), min(end, first + total.shape[1])
            if low < high:
                out.append((source, low - start, total, low - first, high - low))
            first += total.shape[1]
        start = end
    return out


def make_plan(axis, tile_count, tasks, plan):
    odd = lax.rem(lax.axis_index(axis), 2)
    first = lax.axis_index(axis) * tile_count
    last = plan.shape[1] - 1
    for which in range(LISTS):
        plan[which, last] = 0

    def place(tile):
        own = tile - first
        below = own < 0
        above = own >= tile_count
        crossing = jnp.logical_or(
            jnp.logical_and(below, odd == 0), jnp.logical_and(above, odd == 1)
        )
        slot = jnp.where(below, own + HALO, jnp.where(above, own - tile_count, own))
        kind = jnp.where(crossing, CROSS, jnp.where(jnp.logical_or(below, above), CHIP, OWN))
        return slot, kind

    def one(k, carry):
        src, src_kind = place(tasks[0, k])
        dst, dst_kind = place(tasks[1, k])
        which = 3 * src_kind + dst_kind
        count = plan[which, last]
        plan[which, count] = k * 256 + src * 16 + dst
        plan[which, last] = count + 1
        return carry

    ends = []
    size = tasks.shape[1] // GROUPS
    for group in range(GROUPS):
        lax.fori_loop(group * size, (group + 1) * size, one, 0)
        ends.append([plan[3 * OWN + kind, last] for kind in (OWN, CHIP, CROSS)])
    return ends


def edges(axis, tile_count):
    odd = lax.rem(lax.axis_index(axis), 2)
    edge = tile_count - HALO
    return odd * edge, (1 - odd) * edge


def pick_kernel(axis, near_rows, far_rows, amplitudes, *refs):
    *picked, sems = refs
    near, far = edges(axis, amplitudes.shape[0])
    copies = []
    for first, some in ((near, near_rows), (far, far_rows)):
        for rows in some:
            i = len(copies)
            block = amplitudes.at[pl.ds(first, HALO), pl.ds(*rows)]
            copies.append(pltpu.make_async_copy(block, picked[i], sems.at[i]))
            copies[-1].start()
    for copy in copies:
        copy.wait()


def first_kernel(axis, tasks, amplitudes, integrals, plan, own, held, chip_sums, *refs):
    *sums, sems = refs
    size = integrals.shape[0] // GROUPS
    copies = [pltpu.make_async_copy(amplitudes, own, sems.at[GROUPS])]
    for group in range(GROUPS):
        tasks_in_it = pl.ds(group * size, size)
        copies.append(
            pltpu.make_async_copy(
                integrals.at[tasks_in_it], held.at[tasks_in_it], sems.at[group]
            )
        )
    for copy in copies:
        copy.start()
    ends = make_plan(axis, amplitudes.shape[0], tasks, plan)
    for ref in [chip_sums, *sums]:
        ref[...] = jnp.zeros_like(ref)
    copies[0].wait()
    begins = [0] * 3
    for copy, now in zip(copies[1:], ends):
        copy.wait()
        for kind, totals in ((CROSS, sums), (CHIP, [chip_sums])):
            segments = overlaps([own], totals)
            accumulate(plan, 3 * OWN + kind, held, segments, begins[kind], now[kind])
        begins = now


def chip_rims_kernel(parts, plan, integrals, *refs):
    chip, refs = refs[:parts], refs[parts:]
    chip_total, *totals = refs[len(refs) // 2 :]
    accumulate(plan, 3 * CHIP + CROSS, integrals, overlaps(chip, totals))
    accumulate(plan, 3 * CHIP + CHIP, integrals, overlaps(chip, [chip_total]))


def cross_kernel(plan, integrals, sums, halo, total, rim):
    accumulate(plan, 3 * CROSS + CROSS, integrals, overlaps([halo], [total]))
    rim[...] = total[...].astype(rim.dtype)


def rims_kernel(count, chip_chunks, plan, integrals, chip_sums, *refs):
    halos, refs = refs[:count], refs[count:]
    parts = len(chip_chunks)
    more = (len(refs) - parts - 1) // 3
    chip_rims, chip_total = refs[more : more + parts], refs[more + parts]
    totals, rims = refs[more + parts + 1 : -more], refs[-more:]
    accumulate(plan, 3 * CROSS + CROSS, integrals, overlaps([halos[-1]], totals))
    for rim, total in zip(rims, totals):
        rim[...] = total[...].astype(rim.dtype)
    accumulate(plan, 3 * CROSS + CHIP, integrals, overlaps(halos, [chip_total]))
    for (start, size), chip_rim in zip(chip_chunks, chip_rims):
        chip_rim[...] = chip_total[:, pl.ds(start, size)].astype(chip_rim.dtype)


def own_kernel(plan, own, integrals, *refs):
    *chip, total = refs
    total[...] = jnp.zeros_like(total)
    accumulate(plan, 3 * OWN + OWN, integrals, overlaps([own], [total]))
    accumulate(plan, 3 * CHIP + OWN, integrals, overlaps(chip, [total]))


def resident_kernel(plan, integrals, sums, *refs):
    *halos, total = refs
    accumulate(plan, 3 * CROSS + OWN, integrals, overlaps(halos, [total]))


def add_rim(places, sums, out, sems):
    copies = []
    for first, rims, begin, part, sem in places:
        row = 0
        for rim in rims:
            size = rim.shape[1]
            here, there = pl.ds(row, size), pl.ds(begin + row, size)
            for j in range(HALO):
                part[j, here] = sums[first + j, there] + rim[j].astype(jnp.float32)
            copies.append(
                pltpu.make_async_copy(
                    part.at[:, here], out.at[pl.ds(first, HALO), there], sems.at[sem]
                )
            )
            copies[-1].start()
            sem += 1
            row += size
    for copy in copies:
        copy.wait()


def rest_kernel(axis, parts, sums, *refs):
    rims, (out, part, sems) = refs[:-3], refs[-3:]
    near, far = edges(axis, out.shape[0])
    places = [
        (far, rims[:parts], 0, part.at[pl.ds(0, HALO)], 0),
        (near, rims[parts:], 0, part.at[pl.ds(HALO, HALO)], parts),
    ]
    add_rim(places, sums, out, sems)


def last_kernel(axis, begin, sums, rim, before, out, part, sems):
    near, _ = edges(axis, out.shape[0])
    add_rim([(near, [rim], begin, part, 0)], sums, out, sems)


def on_device(amplitudes, integrals, tasks):
    tile_count, rows, width = amplitudes.shape
    task_count = integrals.shape[0]
    chunks = row_chunks(rows, SPLIT)
    rim_chunks = row_chunks(rows, RIM_SPLIT)
    chip_chunks = row_chunks(rows, CHIP_SPLIT)
    chip_rim_chunks = row_chunks(rows, CHIP_RIM_SPLIT)
    count = len(chunks)
    many = len(rim_chunks)
    axis = "own"
    devices = lax.axis_size(axis)
    cross_pairs = [(i, i + 1) for i in range(1, devices - 1, 2)]
    cross_pairs += [(b, a) for a, b in cross_pairs]
    chip_pairs = [(i, i ^ 1) for i in range(devices)]
    f32, bf16, i32 = jnp.float32, amplitudes.dtype, jnp.int32

    def call(kernel, name, operands, in_specs, after=(), **kwargs):
        here = len(operands)

        def body(*refs):
            kernel(*refs[:here], *refs[here + len(after) :])

        return pl.pallas_call(
            body,
            in_specs=in_specs + [pl.BlockSpec(memory_space=pl.ANY)] * len(after),
            compiler_params=pltpu.CompilerParams(vmem_limit_bytes=VMEM_LIMIT),
            cost_estimate=pl.CostEstimate(flops=1, bytes_accessed=1, transcendentals=0),
            name=name,
            **kwargs,
        )(*operands, *after)

    def swap_cross(x):
        return in_vmem(lax.ppermute(x, axis, cross_pairs))

    def swap_chip(x):
        return in_vmem(lax.ppermute(x, axis, chip_pairs))

    amplitudes, integrals = in_hbm(amplitudes), in_hbm(integrals)
    def pick(near_rows, far_rows, after=()):
        sizes = [size for _, size in near_rows + far_rows]
        return call(
            functools.partial(pick_kernel, axis, near_rows, far_rows),
            "pick",
            [amplitudes],
            [hbm()],
            after=after,
            out_shape=[jax.ShapeDtypeStruct((HALO, size, width), bf16) for size in sizes],
            out_specs=[hbm()] * len(sizes),
            scratch_shapes=[pltpu.SemaphoreType.DMA((len(sizes),))],
        )

    parts = len(chip_chunks)
    head = pick(chunks[:1], [])
    rest = pick(chunks[1:], chip_chunks, after=head)
    halos = [swap_cross(x) for x in head + rest[: count - 1]]
    chip_halos = [swap_chip(x) for x in rest[count - 1 :]]

    edge_shape = pltpu.VMEM((HALO, rows, width), f32)
    sums_shapes = [edge_shape] + [pltpu.VMEM((HALO, size, width), f32) for _, size in rim_chunks]
    plan, own, held, *sums = call(
        functools.partial(first_kernel, axis),
        "own_rims",
        [tasks.T, amplitudes, integrals],
        [smem(), hbm(), hbm()],
        after=rest,
        out_shape=[
            jax.ShapeDtypeStruct((LISTS, task_count + 1), i32),
            pltpu.VMEM(amplitudes.shape, bf16),
            pltpu.VMEM(integrals.shape, bf16),
        ]
        + sums_shapes,
        out_specs=[smem()] + [vmem()] * (3 + many),
        scratch_shapes=[pltpu.SemaphoreType.DMA((1 + GROUPS,))],
    )
    own, held = in_vmem(own), in_vmem(held)
    chip_sums, *cross_sums = call(
        functools.partial(chip_rims_kernel, parts),
        "chip_rims",
        [plan, held, *chip_halos, *[in_vmem(x) for x in sums]],
        [smem()] + [vmem()] * (many + 2 + parts),
        out_shape=sums_shapes,
        out_specs=[vmem()] * (many + 1),
        input_output_aliases={2 + parts + i: i for i in range(many + 1)},
    )
    chip_sums = in_vmem(chip_sums)

    rims = []
    after = ()
    for i in range(count - 1):
        size = chunks[i][1]
        _, rim = call(
            cross_kernel,
            "cross_rim",
            [plan, held, in_vmem(cross_sums[i]), halos[i]],
            [smem()] + [vmem()] * 3,
            after=after,
            out_shape=[
                pltpu.VMEM((HALO, size, width), f32),
                pltpu.VMEM((HALO, size, width), bf16),
            ],
            out_specs=[vmem()] * 2,
            input_output_aliases={2: 0},
        )
        rims.append(rim)
        after = [in_vmem(rim)]
    resident_shape = pltpu.VMEM((tile_count, rows, width), f32)
    resident = call(
        own_kernel,
        "own_targets",
        [plan, own, held, *chip_halos],
        [smem()] + [vmem()] * (2 + parts),
        after=after,
        out_shape=resident_shape,
        out_specs=vmem(),
    )
    resident = in_vmem(resident)
    more = many - count + 1
    chip_parts = len(chip_rim_chunks)
    last = [pltpu.VMEM((HALO, size, width), bf16) for _, size in rim_chunks[-more:]]
    got = call(
        functools.partial(rims_kernel, count, chip_rim_chunks),
        "last_rims",
        [plan, held, chip_sums, *halos, *[in_vmem(x) for x in cross_sums[-more:]]],
        [smem()] + [vmem()] * (2 + count + more),
        after=[resident],
        out_shape=[pltpu.VMEM((HALO, size, width), bf16) for _, size in chip_rim_chunks]
        + [edge_shape]
        + [pltpu.VMEM((HALO, size, width), f32) for _, size in rim_chunks[-more:]]
        + last,
        out_specs=[vmem()] * (chip_parts + 1 + 2 * more),
        input_output_aliases={2: chip_parts}
        | {3 + count + i: chip_parts + 1 + i for i in range(more)},
    )
    chip_rims, rim = got[:chip_parts], got[-1]
    rims += got[-more:]
    from_chip = [swap_chip(x) for x in chip_rims]
    from_cross = [swap_cross(x) for x in rims]
    resident = call(
        resident_kernel,
        "cross_sources",
        [plan, held, resident, *halos],
        [smem()] + [vmem()] * (2 + count),
        after=[in_vmem(rim)],
        out_shape=resident_shape,
        out_specs=vmem(),
        input_output_aliases={2: 0},
    )
    resident = in_vmem(resident)

    shape = jax.ShapeDtypeStruct((tile_count, rows, width), f32)
    blocks = from_chip + from_cross[:1]
    out = call(
        functools.partial(rest_kernel, axis, chip_parts),
        "residual",
        [resident, *blocks],
        [vmem()] * (1 + len(blocks)),
        out_shape=shape,
        out_specs=hbm(),
        scratch_shapes=[
            pltpu.VMEM((2 * HALO, rows, width), f32),
            pltpu.SemaphoreType.DMA((len(blocks),)),
        ],
    )
    for (begin, size), rim in zip(rim_chunks[1:], from_cross[1:]):
        out = call(
            functools.partial(last_kernel, axis, begin),
            "residual_last",
            [resident, rim, out],
            [vmem()] * 2 + [hbm()],
            out_shape=shape,
            out_specs=hbm(),
            scratch_shapes=[
                pltpu.VMEM((HALO, size, width), f32),
                pltpu.SemaphoreType.DMA((1,)),
            ],
            input_output_aliases={2: 0},
        )
    return out


def solution(mesh):
    return jax.shard_map(
        on_device,
        mesh=mesh,
        in_specs=(
            P(("parts", "own"), None, None),
            P(("parts", "own"), None, None),
            P(("parts", "own"), None),
        ),
        out_specs=P(("parts", "own"), None, None),
        check_vma=False,
    )
```

```python
import functools

import jax
import jax.numpy as jnp
from jax import lax
from jax.experimental import pallas as pl
from jax.experimental.pallas import tpu as pltpu
from jax.sharding import PartitionSpec as P

HALO = 2
SPLIT = (512, 512)
RIM_SPLIT = (512, 432, 80)
CHIP_RIM_SPLIT = (352, 336, 336)
CHIP_SPLIT = (384, 384, 256)
VMEM_LIMIT = 24 * 1024 * 1024

OWN, CHIP, CROSS = 0, 1, 2
LISTS = 9
GROUPS = 3


def row_chunks(rows, split):
    total = sum(split)
    sizes = [rows * part // total for part in split]
    starts = [sum(sizes[:i]) for i in range(len(sizes))]
    return list(zip(starts, sizes))


def vmem():
    return pl.BlockSpec(memory_space=pltpu.VMEM)


def smem():
    return pl.BlockSpec(memory_space=pltpu.SMEM)


def hbm():
    return pl.BlockSpec(memory_space=pltpu.HBM)


def in_vmem(x):
    return pltpu.with_memory_space_constraint(x, pltpu.VMEM)


def in_hbm(x):
    return pltpu.with_memory_space_constraint(x, pltpu.HBM)


def accumulate(plan, which, integrals, segments, begin=0, end=None):
    end = plan[which, plan.shape[1] - 1] if end is None else end

    def some(first, width):
        entries = [plan[which, first + u] for u in range(width)]
        for source, low, sums, offset, size in segments:
            for r in range(0, size, 256):
                block = min(256, size - r)
                products = [
                    jnp.dot(
                        source[(entry >> 4) & 15, pl.ds(low + r, block)],
                        integrals[entry >> 8],
                        preferred_element_type=jnp.float32,
                    )
                    for entry in entries
                ]
                for entry, product in zip(entries, products):
                    sums[entry & 15, pl.ds(offset + r, block)] += product

    def pair(i, carry):
        some(begin + 2 * i, 2)
        return carry

    def single(i, carry):
        some(i, 1)
        return carry

    pairs = (end - begin) // 2
    lax.fori_loop(0, pairs, pair, 0)
    lax.fori_loop(begin + 2 * pairs, end, single, 0)


def overlaps(sources, totals):
    out = []
    start = 0
    for source in sources:
        end = start + source.shape[1]
        first = 0
        for total in totals:
            low, high = max(start, first), min(end, first + total.shape[1])
            if low < high:
                out.append((source, low - start, total, low - first, high - low))
            first += total.shape[1]
        start = end
    return out


def make_plan(axis, tile_count, tasks, plan):
    odd = lax.rem(lax.axis_index(axis), 2)
    first = lax.axis_index(axis) * tile_count
    last = plan.shape[1] - 1
    for which in range(LISTS):
        plan[which, last] = 0

    def place(tile):
        own = tile - first
        below = own < 0
        above = own >= tile_count
        crossing = jnp.logical_or(
            jnp.logical_and(below, odd == 0), jnp.logical_and(above, odd == 1)
        )
        slot = jnp.where(below, own + HALO, jnp.where(above, own - tile_count, own))
        kind = jnp.where(crossing, CROSS, jnp.where(jnp.logical_or(below, above), CHIP, OWN))
        return slot, kind

    def one(k, carry):
        src, src_kind = place(tasks[0, k])
        dst, dst_kind = place(tasks[1, k])
        which = 3 * src_kind + dst_kind
        count = plan[which, last]
        plan[which, count] = k * 256 + src * 16 + dst
        plan[which, last] = count + 1
        return carry

    ends = []
    size = tasks.shape[1] // GROUPS
    for group in range(GROUPS):
        lax.fori_loop(group * size, (group + 1) * size, one, 0)
        ends.append([plan[3 * OWN + kind, last] for kind in (OWN, CHIP, CROSS)])
    return ends


def edges(axis, tile_count):
    odd = lax.rem(lax.axis_index(axis), 2)
    edge = tile_count - HALO
    return odd * edge, (1 - odd) * edge


def pick_kernel(axis, near_rows, far_rows, amplitudes, *refs):
    *picked, sems = refs
    near, far = edges(axis, amplitudes.shape[0])
    copies = []
    for first, some in ((near, near_rows), (far, far_rows)):
        for rows in some:
            i = len(copies)
            block = amplitudes.at[pl.ds(first, HALO), pl.ds(*rows)]
            copies.append(pltpu.make_async_copy(block, picked[i], sems.at[i]))
            copies[-1].start()
    for copy in copies:
        copy.wait()


def first_kernel(axis, tasks, amplitudes, integrals, plan, own, held, chip_sums, *refs):
    *sums, sems = refs
    size = integrals.shape[0] // GROUPS
    copies = [pltpu.make_async_copy(amplitudes, own, sems.at[GROUPS])]
    for group in range(GROUPS):
        tasks_in_it = pl.ds(group * size, size)
        copies.append(
            pltpu.make_async_copy(
                integrals.at[tasks_in_it], held.at[tasks_in_it], sems.at[group]
            )
        )
    for copy in copies:
        copy.start()
    ends = make_plan(axis, amplitudes.shape[0], tasks, plan)
    for ref in [chip_sums, *sums]:
        ref[...] = jnp.zeros_like(ref)
    copies[0].wait()
    begins = [0] * 3
    for copy, now in zip(copies[1:], ends):
        copy.wait()
        for kind, totals in ((CROSS, sums), (CHIP, [chip_sums])):
            segments = overlaps([own], totals)
            accumulate(plan, 3 * OWN + kind, held, segments, begins[kind], now[kind])
        begins = now


def chip_rims_kernel(parts, plan, integrals, *refs):
    chip, refs = refs[:parts], refs[parts:]
    chip_total, *totals = refs[len(refs) // 2 :]
    accumulate(plan, 3 * CHIP + CROSS, integrals, overlaps(chip, totals))
    accumulate(plan, 3 * CHIP + CHIP, integrals, overlaps(chip, [chip_total]))


def cross_kernel(plan, integrals, sums, halo, total, rim):
    accumulate(plan, 3 * CROSS + CROSS, integrals, overlaps([halo], [total]))
    rim[...] = total[...].astype(rim.dtype)


def rims_kernel(count, chip_chunks, plan, integrals, chip_sums, *refs):
    halos, refs = refs[:count], refs[count:]
    parts = len(chip_chunks)
    more = (len(refs) - parts - 1) // 3
    chip_rims, chip_total = refs[more : more + parts], refs[more + parts]
    totals, rims = refs[more + parts + 1 : -more], refs[-more:]
    accumulate(plan, 3 * CROSS + CROSS, integrals, overlaps([halos[-1]], totals))
    for rim, total in zip(rims, totals):
        rim[...] = total[...].astype(rim.dtype)
    accumulate(plan, 3 * CROSS + CHIP, integrals, overlaps(halos, [chip_total]))
    for (start, size), chip_rim in zip(chip_chunks, chip_rims):
        chip_rim[...] = chip_total[:, pl.ds(start, size)].astype(chip_rim.dtype)


def own_kernel(plan, own, integrals, *refs):
    *chip, total = refs
    total[...] = jnp.zeros_like(total)
    accumulate(plan, 3 * OWN + OWN, integrals, overlaps([own], [total]))
    accumulate(plan, 3 * CHIP + OWN, integrals, overlaps(chip, [total]))


def resident_kernel(plan, integrals, sums, *refs):
    *halos, total = refs
    accumulate(plan, 3 * CROSS + OWN, integrals, overlaps(halos, [total]))


def pass_kernel(block, same):
    pass


def add_rim(places, sums, out, sems):
    copies = []
    for first, rims, begin, part, sem in places:
        row = 0
        for rim in rims:
            size = rim.shape[1]
            here, there = pl.ds(row, size), pl.ds(begin + row, size)
            for j in range(HALO):
                part[j, here] = sums[first + j, there] + rim[j].astype(jnp.float32)
            copies.append(
                pltpu.make_async_copy(
                    part.at[:, here], out.at[pl.ds(first, HALO), there], sems.at[sem]
                )
            )
            copies[-1].start()
            sem += 1
            row += size
    for copy in copies:
        copy.wait()


def rest_kernel(axis, parts, sums, *refs):
    rims, (out, part, sems) = refs[:-3], refs[-3:]
    near, far = edges(axis, out.shape[0])
    places = [
        (far, rims[:parts], 0, part.at[pl.ds(0, HALO)], 0),
        (near, rims[parts:], 0, part.at[pl.ds(HALO, HALO)], parts),
    ]
    add_rim(places, sums, out, sems)


def last_kernel(axis, begin, sums, rim, before, out, part, sems):
    near, _ = edges(axis, out.shape[0])
    add_rim([(near, [rim], begin, part, 0)], sums, out, sems)


def on_device(amplitudes, integrals, tasks):
    tile_count, rows, width = amplitudes.shape
    task_count = integrals.shape[0]
    chunks = row_chunks(rows, SPLIT)
    rim_chunks = row_chunks(rows, RIM_SPLIT)
    chip_chunks = row_chunks(rows, CHIP_SPLIT)
    chip_rim_chunks = row_chunks(rows, CHIP_RIM_SPLIT)
    count = len(chunks)
    many = len(rim_chunks)
    axis = "own"
    devices = lax.axis_size(axis)
    cross_pairs = [(i, i + 1) for i in range(1, devices - 1, 2)]
    cross_pairs += [(b, a) for a, b in cross_pairs]
    chip_pairs = [(i, i ^ 1) for i in range(devices)]
    f32, bf16, i32 = jnp.float32, amplitudes.dtype, jnp.int32

    def call(kernel, name, operands, in_specs, after=(), **kwargs):
        here = len(operands)

        def body(*refs):
            kernel(*refs[:here], *refs[here + len(after) :])

        return pl.pallas_call(
            body,
            in_specs=in_specs + [pl.BlockSpec(memory_space=pl.ANY)] * len(after),
            compiler_params=pltpu.CompilerParams(vmem_limit_bytes=VMEM_LIMIT),
            cost_estimate=pl.CostEstimate(flops=1, bytes_accessed=1, transcendentals=0),
            name=name,
            **kwargs,
        )(*operands, *after)

    def swap_cross(x):
        return in_vmem(lax.ppermute(x, axis, cross_pairs))

    def swap_chip(x):
        return in_vmem(lax.ppermute(x, axis, chip_pairs))

    amplitudes, integrals = in_hbm(amplitudes), in_hbm(integrals)
    def pick(near_rows, far_rows, after=()):
        sizes = [size for _, size in near_rows + far_rows]
        return call(
            functools.partial(pick_kernel, axis, near_rows, far_rows),
            "pick",
            [amplitudes],
            [hbm()],
            after=after,
            out_shape=[pltpu.VMEM((HALO, size, width), bf16) for size in sizes],
            out_specs=[vmem()] * len(sizes),
            scratch_shapes=[pltpu.SemaphoreType.DMA((len(sizes),))],
        )

    parts = len(chip_chunks)
    head = pick(chunks[:1], [])
    rest = pick(chunks[1:], chip_chunks, after=head)
    halos = [swap_cross(x) for x in head + rest[: count - 1]]
    chip_halos = [swap_chip(x) for x in rest[count - 1 :]]

    edge_shape = pltpu.VMEM((HALO, rows, width), f32)
    sums_shapes = [edge_shape] + [pltpu.VMEM((HALO, size, width), f32) for _, size in rim_chunks]
    plan, own, held, *sums = call(
        functools.partial(first_kernel, axis),
        "own_rims",
        [tasks.T, amplitudes, integrals],
        [smem(), hbm(), hbm()],
        after=rest,
        out_shape=[
            jax.ShapeDtypeStruct((LISTS, task_count + 1), i32),
            pltpu.VMEM(amplitudes.shape, bf16),
            pltpu.VMEM(integrals.shape, bf16),
        ]
        + sums_shapes,
        out_specs=[smem()] + [vmem()] * (3 + many),
        scratch_shapes=[pltpu.SemaphoreType.DMA((1 + GROUPS,))],
    )
    own, held = in_vmem(own), in_vmem(held)
    chip_sums, *cross_sums = call(
        functools.partial(chip_rims_kernel, parts),
        "chip_rims",
        [plan, held, *chip_halos, *[in_vmem(x) for x in sums]],
        [smem()] + [vmem()] * (many + 2 + parts),
        out_shape=sums_shapes,
        out_specs=[vmem()] * (many + 1),
        input_output_aliases={2 + parts + i: i for i in range(many + 1)},
    )
    chip_sums = in_vmem(chip_sums)

    rims = []
    after = ()
    for i in range(count - 1):
        size = chunks[i][1]
        _, rim = call(
            cross_kernel,
            "cross_rim",
            [plan, held, in_vmem(cross_sums[i]), halos[i]],
            [smem()] + [vmem()] * 3,
            after=after,
            out_shape=[
                pltpu.VMEM((HALO, size, width), f32),
                pltpu.VMEM((HALO, size, width), bf16),
            ],
            out_specs=[vmem()] * 2,
            input_output_aliases={2: 0},
        )
        rims.append(rim)
        after = [in_vmem(rim)]
    resident_shape = pltpu.VMEM((tile_count, rows, width), f32)
    resident = call(
        own_kernel,
        "own_targets",
        [plan, own, held, *chip_halos],
        [smem()] + [vmem()] * (2 + parts),
        after=after,
        out_shape=resident_shape,
        out_specs=vmem(),
    )
    resident = in_vmem(resident)
    more = many - count + 1
    chip_parts = len(chip_rim_chunks)
    last = [pltpu.VMEM((HALO, size, width), bf16) for _, size in rim_chunks[-more:]]
    got = call(
        functools.partial(rims_kernel, count, chip_rim_chunks),
        "last_rims",
        [plan, held, chip_sums, *halos, *[in_vmem(x) for x in cross_sums[-more:]]],
        [smem()] + [vmem()] * (2 + count + more),
        after=[resident],
        out_shape=[pltpu.VMEM((HALO, size, width), bf16) for _, size in chip_rim_chunks]
        + [edge_shape]
        + [pltpu.VMEM((HALO, size, width), f32) for _, size in rim_chunks[-more:]]
        + last,
        out_specs=[vmem()] * (chip_parts + 1 + 2 * more),
        input_output_aliases={2: chip_parts}
        | {3 + count + i: chip_parts + 1 + i for i in range(more)},
    )
    chip_rims, rim = got[:chip_parts], got[-1]
    rims += got[-more:]
    from_chip = [swap_chip(x) for x in chip_rims]
    from_cross = [swap_cross(x) for x in rims[:-1]]
    resident = call(
        resident_kernel,
        "cross_sources",
        [plan, held, resident, *halos],
        [smem()] + [vmem()] * (2 + count),
        after=[in_vmem(rims[-2])],
        out_shape=resident_shape,
        out_specs=vmem(),
        input_output_aliases={2: 0},
    )
    resident = in_vmem(resident)
    rim = call(
        pass_kernel,
        "pass_on",
        [in_vmem(rim)],
        [vmem()],
        after=[resident],
        out_shape=pltpu.VMEM(rim.shape, bf16),
        out_specs=vmem(),
        input_output_aliases={0: 0},
    )
    from_cross.append(swap_cross(rim))

    shape = jax.ShapeDtypeStruct((tile_count, rows, width), f32)
    blocks = from_chip + from_cross[:1]
    out = call(
        functools.partial(rest_kernel, axis, chip_parts),
        "residual",
        [resident, *blocks],
        [vmem()] * (1 + len(blocks)),
        out_shape=shape,
        out_specs=hbm(),
        scratch_shapes=[
            pltpu.VMEM((2 * HALO, rows, width), f32),
            pltpu.SemaphoreType.DMA((len(blocks),)),
        ],
    )
    for (begin, size), rim in zip(rim_chunks[1:], from_cross[1:]):
        out = call(
            functools.partial(last_kernel, axis, begin),
            "residual_last",
            [resident, rim, out],
            [vmem()] * 2 + [hbm()],
            out_shape=shape,
            out_specs=hbm(),
            scratch_shapes=[
                pltpu.VMEM((HALO, size, width), f32),
                pltpu.SemaphoreType.DMA((1,)),
            ],
            input_output_aliases={2: 0},
        )
    return out


def solution(mesh):
    return jax.shard_map(
        on_device,
        mesh=mesh,
        in_specs=(
            P(("parts", "own"), None, None),
            P(("parts", "own"), None, None),
            P(("parts", "own"), None),
        ),
        out_specs=P(("parts", "own"), None, None),
        check_vma=False,
    )
```

```python
import functools

import jax
import jax.numpy as jnp
from jax import lax
from jax.experimental import pallas as pl
from jax.experimental.pallas import tpu as pltpu
from jax.sharding import PartitionSpec as P

HALO = 2
SPLIT = (496, 528)
RIM_SPLIT = (496, 432, 96)
CHIP_RIM_SPLIT = (352, 336, 336)
CHIP_SPLIT = (384, 384, 256)
VMEM_LIMIT = 24 * 1024 * 1024

OWN, CHIP, CROSS = 0, 1, 2
LISTS = 9
GROUPS = 3


def row_chunks(rows, split):
    total = sum(split)
    sizes = [rows * part // total for part in split]
    starts = [sum(sizes[:i]) for i in range(len(sizes))]
    return list(zip(starts, sizes))


def vmem():
    return pl.BlockSpec(memory_space=pltpu.VMEM)


def smem():
    return pl.BlockSpec(memory_space=pltpu.SMEM)


def hbm():
    return pl.BlockSpec(memory_space=pltpu.HBM)


def in_vmem(x):
    return pltpu.with_memory_space_constraint(x, pltpu.VMEM)


def in_hbm(x):
    return pltpu.with_memory_space_constraint(x, pltpu.HBM)


def accumulate(plan, which, integrals, segments, begin=0, end=None):
    end = plan[which, plan.shape[1] - 1] if end is None else end

    def some(first, width):
        entries = [plan[which, first + u] for u in range(width)]
        for source, low, sums, offset, size in segments:
            for r in range(0, size, 256):
                block = min(256, size - r)
                products = [
                    jnp.dot(
                        source[(entry >> 4) & 15, pl.ds(low + r, block)],
                        integrals[entry >> 8],
                        preferred_element_type=jnp.float32,
                    )
                    for entry in entries
                ]
                for entry, product in zip(entries, products):
                    sums[entry & 15, pl.ds(offset + r, block)] += product

    def pair(i, carry):
        some(begin + 2 * i, 2)
        return carry

    def single(i, carry):
        some(i, 1)
        return carry

    pairs = (end - begin) // 2
    lax.fori_loop(0, pairs, pair, 0)
    lax.fori_loop(begin + 2 * pairs, end, single, 0)


def overlaps(sources, totals):
    out = []
    start = 0
    for source in sources:
        end = start + source.shape[1]
        first = 0
        for total in totals:
            low, high = max(start, first), min(end, first + total.shape[1])
            if low < high:
                out.append((source, low - start, total, low - first, high - low))
            first += total.shape[1]
        start = end
    return out


def make_plan(axis, tile_count, tasks, plan):
    odd = lax.rem(lax.axis_index(axis), 2)
    first = lax.axis_index(axis) * tile_count
    last = plan.shape[1] - 1
    for which in range(LISTS):
        plan[which, last] = 0

    def place(tile):
        own = tile - first
        below = own < 0
        above = own >= tile_count
        crossing = jnp.logical_or(
            jnp.logical_and(below, odd == 0), jnp.logical_and(above, odd == 1)
        )
        slot = jnp.where(below, own + HALO, jnp.where(above, own - tile_count, own))
        kind = jnp.where(crossing, CROSS, jnp.where(jnp.logical_or(below, above), CHIP, OWN))
        return slot, kind

    def one(k, carry):
        src, src_kind = place(tasks[0, k])
        dst, dst_kind = place(tasks[1, k])
        which = 3 * src_kind + dst_kind
        count = plan[which, last]
        plan[which, count] = k * 256 + src * 16 + dst
        plan[which, last] = count + 1
        return carry

    ends = []
    size = tasks.shape[1] // GROUPS
    for group in range(GROUPS):
        lax.fori_loop(group * size, (group + 1) * size, one, 0)
        ends.append([plan[3 * OWN + kind, last] for kind in (OWN, CHIP, CROSS)])
    return ends


def edges(axis, tile_count):
    odd = lax.rem(lax.axis_index(axis), 2)
    edge = tile_count - HALO
    return odd * edge, (1 - odd) * edge


def pick_kernel(axis, near_rows, far_rows, amplitudes, *refs):
    *picked, sems = refs
    near, far = edges(axis, amplitudes.shape[0])
    copies = []
    for first, some in ((near, near_rows), (far, far_rows)):
        for rows in some:
            i = len(copies)
            block = amplitudes.at[pl.ds(first, HALO), pl.ds(*rows)]
            copies.append(pltpu.make_async_copy(block, picked[i], sems.at[i]))
            copies[-1].start()
    for copy in copies:
        copy.wait()


def first_kernel(axis, tasks, amplitudes, integrals, plan, own, held, chip_sums, *refs):
    *sums, sems = refs
    size = integrals.shape[0] // GROUPS
    copies = [pltpu.make_async_copy(amplitudes, own, sems.at[GROUPS])]
    for group in range(GROUPS):
        tasks_in_it = pl.ds(group * size, size)
        copies.append(
            pltpu.make_async_copy(
                integrals.at[tasks_in_it], held.at[tasks_in_it], sems.at[group]
            )
        )
    for copy in copies:
        copy.start()
    ends = make_plan(axis, amplitudes.shape[0], tasks, plan)
    for ref in [chip_sums, *sums]:
        ref[...] = jnp.zeros_like(ref)
    copies[0].wait()
    begins = [0] * 3
    for copy, now in zip(copies[1:], ends):
        copy.wait()
        for kind, totals in ((CROSS, sums), (CHIP, [chip_sums])):
            segments = overlaps([own], totals)
            accumulate(plan, 3 * OWN + kind, held, segments, begins[kind], now[kind])
        begins = now


def chip_rims_kernel(parts, plan, integrals, *refs):
    chip, refs = refs[:parts], refs[parts:]
    chip_total, *totals = refs[len(refs) // 2 :]
    accumulate(plan, 3 * CHIP + CROSS, integrals, overlaps(chip, totals))
    accumulate(plan, 3 * CHIP + CHIP, integrals, overlaps(chip, [chip_total]))


def cross_kernel(plan, integrals, sums, halo, total, rim):
    accumulate(plan, 3 * CROSS + CROSS, integrals, overlaps([halo], [total]))
    rim[...] = total[...].astype(rim.dtype)


def rims_kernel(count, chip_chunks, plan, integrals, chip_sums, *refs):
    halos, refs = refs[:count], refs[count:]
    parts = len(chip_chunks)
    more = (len(refs) - parts - 1) // 3
    chip_rims, chip_total = refs[more : more + parts], refs[more + parts]
    totals, rims = refs[more + parts + 1 : -more], refs[-more:]
    accumulate(plan, 3 * CROSS + CROSS, integrals, overlaps([halos[-1]], totals))
    for rim, total in zip(rims, totals):
        rim[...] = total[...].astype(rim.dtype)
    accumulate(plan, 3 * CROSS + CHIP, integrals, overlaps(halos, [chip_total]))
    for (start, size), chip_rim in zip(chip_chunks, chip_rims):
        chip_rim[...] = chip_total[:, pl.ds(start, size)].astype(chip_rim.dtype)


def own_kernel(plan, own, integrals, *refs):
    *chip, total = refs
    total[...] = jnp.zeros_like(total)
    accumulate(plan, 3 * OWN + OWN, integrals, overlaps([own], [total]))
    accumulate(plan, 3 * CHIP + OWN, integrals, overlaps(chip, [total]))


def resident_kernel(plan, integrals, sums, *refs):
    *halos, total = refs
    accumulate(plan, 3 * CROSS + OWN, integrals, overlaps(halos, [total]))


def pass_kernel(block, same):
    pass


def add_rim(places, sums, out, sems):
    copies = []
    for first, rims, begin, part, sem in places:
        row = 0
        for rim in rims:
            size = rim.shape[1]
            here, there = pl.ds(row, size), pl.ds(begin + row, size)
            for j in range(HALO):
                part[j, here] = sums[first + j, there] + rim[j].astype(jnp.float32)
            copies.append(
                pltpu.make_async_copy(
                    part.at[:, here], out.at[pl.ds(first, HALO), there], sems.at[sem]
                )
            )
            copies[-1].start()
            sem += 1
            row += size
    for copy in copies:
        copy.wait()


def rest_kernel(axis, parts, sums, *refs):
    rims, (out, part, sems) = refs[:-3], refs[-3:]
    near, far = edges(axis, out.shape[0])
    places = [
        (far, rims[:parts], 0, part.at[pl.ds(0, HALO)], 0),
        (near, rims[parts:], 0, part.at[pl.ds(HALO, HALO)], parts),
    ]
    add_rim(places, sums, out, sems)


def last_kernel(axis, begin, sums, rim, before, out, part, sems):
    near, _ = edges(axis, out.shape[0])
    add_rim([(near, [rim], begin, part, 0)], sums, out, sems)


def on_device(amplitudes, integrals, tasks):
    tile_count, rows, width = amplitudes.shape
    task_count = integrals.shape[0]
    chunks = row_chunks(rows, SPLIT)
    rim_chunks = row_chunks(rows, RIM_SPLIT)
    chip_chunks = row_chunks(rows, CHIP_SPLIT)
    chip_rim_chunks = row_chunks(rows, CHIP_RIM_SPLIT)
    count = len(chunks)
    many = len(rim_chunks)
    axis = "own"
    devices = lax.axis_size(axis)
    cross_pairs = [(i, i + 1) for i in range(1, devices - 1, 2)]
    cross_pairs += [(b, a) for a, b in cross_pairs]
    chip_pairs = [(i, i ^ 1) for i in range(devices)]
    f32, bf16, i32 = jnp.float32, amplitudes.dtype, jnp.int32

    def call(kernel, name, operands, in_specs, after=(), **kwargs):
        here = len(operands)

        def body(*refs):
            kernel(*refs[:here], *refs[here + len(after) :])

        return pl.pallas_call(
            body,
            in_specs=in_specs + [pl.BlockSpec(memory_space=pl.ANY)] * len(after),
            compiler_params=pltpu.CompilerParams(vmem_limit_bytes=VMEM_LIMIT),
            cost_estimate=pl.CostEstimate(flops=1, bytes_accessed=1, transcendentals=0),
            name=name,
            **kwargs,
        )(*operands, *after)

    def swap_cross(x):
        return in_vmem(lax.ppermute(x, axis, cross_pairs))

    def swap_chip(x):
        return in_vmem(lax.ppermute(x, axis, chip_pairs))

    amplitudes, integrals = in_hbm(amplitudes), in_hbm(integrals)
    def pick(near_rows, far_rows, after=()):
        sizes = [size for _, size in near_rows + far_rows]
        return call(
            functools.partial(pick_kernel, axis, near_rows, far_rows),
            "pick",
            [amplitudes],
            [hbm()],
            after=after,
            out_shape=[pltpu.VMEM((HALO, size, width), bf16) for size in sizes],
            out_specs=[vmem()] * len(sizes),
            scratch_shapes=[pltpu.SemaphoreType.DMA((len(sizes),))],
        )

    parts = len(chip_chunks)
    head = pick(chunks[:1], [])
    rest = pick(chunks[1:], chip_chunks, after=head)
    halos = [swap_cross(x) for x in head + rest[: count - 1]]
    chip_halos = [swap_chip(x) for x in rest[count - 1 :]]

    edge_shape = pltpu.VMEM((HALO, rows, width), f32)
    sums_shapes = [edge_shape] + [pltpu.VMEM((HALO, size, width), f32) for _, size in rim_chunks]
    plan, own, held, *sums = call(
        functools.partial(first_kernel, axis),
        "own_rims",
        [tasks.T, amplitudes, integrals],
        [smem(), hbm(), hbm()],
        after=rest,
        out_shape=[
            jax.ShapeDtypeStruct((LISTS, task_count + 1), i32),
            pltpu.VMEM(amplitudes.shape, bf16),
            pltpu.VMEM(integrals.shape, bf16),
        ]
        + sums_shapes,
        out_specs=[smem()] + [vmem()] * (3 + many),
        scratch_shapes=[pltpu.SemaphoreType.DMA((1 + GROUPS,))],
    )
    own, held = in_vmem(own), in_vmem(held)
    chip_sums, *cross_sums = call(
        functools.partial(chip_rims_kernel, parts),
        "chip_rims",
        [plan, held, *chip_halos, *[in_vmem(x) for x in sums]],
        [smem()] + [vmem()] * (many + 2 + parts),
        out_shape=sums_shapes,
        out_specs=[vmem()] * (many + 1),
        input_output_aliases={2 + parts + i: i for i in range(many + 1)},
    )
    chip_sums = in_vmem(chip_sums)

    rims = []
    after = ()
    for i in range(count - 1):
        size = chunks[i][1]
        _, rim = call(
            cross_kernel,
            "cross_rim",
            [plan, held, in_vmem(cross_sums[i]), halos[i]],
            [smem()] + [vmem()] * 3,
            after=after,
            out_shape=[
                pltpu.VMEM((HALO, size, width), f32),
                pltpu.VMEM((HALO, size, width), bf16),
            ],
            out_specs=[vmem()] * 2,
            input_output_aliases={2: 0},
        )
        rims.append(rim)
        after = [in_vmem(rim)]
    resident_shape = pltpu.VMEM((tile_count, rows, width), f32)
    resident = call(
        own_kernel,
        "own_targets",
        [plan, own, held, *chip_halos],
        [smem()] + [vmem()] * (2 + parts),
        after=after,
        out_shape=resident_shape,
        out_specs=vmem(),
    )
    resident = in_vmem(resident)
    more = many - count + 1
    chip_parts = len(chip_rim_chunks)
    last = [pltpu.VMEM((HALO, size, width), bf16) for _, size in rim_chunks[-more:]]
    got = call(
        functools.partial(rims_kernel, count, chip_rim_chunks),
        "last_rims",
        [plan, held, chip_sums, *halos, *[in_vmem(x) for x in cross_sums[-more:]]],
        [smem()] + [vmem()] * (2 + count + more),
        after=[resident],
        out_shape=[pltpu.VMEM((HALO, size, width), bf16) for _, size in chip_rim_chunks]
        + [edge_shape]
        + [pltpu.VMEM((HALO, size, width), f32) for _, size in rim_chunks[-more:]]
        + last,
        out_specs=[vmem()] * (chip_parts + 1 + 2 * more),
        input_output_aliases={2: chip_parts}
        | {3 + count + i: chip_parts + 1 + i for i in range(more)},
    )
    chip_rims, rim = got[:chip_parts], got[-1]
    rims += got[-more:]
    from_chip = [swap_chip(x) for x in chip_rims]
    from_cross = [swap_cross(x) for x in rims[:-1]]
    resident = call(
        resident_kernel,
        "cross_sources",
        [plan, held, resident, *halos],
        [smem()] + [vmem()] * (2 + count),
        after=[in_vmem(rims[-2])],
        out_shape=resident_shape,
        out_specs=vmem(),
        input_output_aliases={2: 0},
    )
    resident = in_vmem(resident)
    rim = call(
        pass_kernel,
        "pass_on",
        [in_vmem(rim)],
        [vmem()],
        after=[resident],
        out_shape=pltpu.VMEM(rim.shape, bf16),
        out_specs=vmem(),
        input_output_aliases={0: 0},
    )
    from_cross.append(swap_cross(rim))

    shape = jax.ShapeDtypeStruct((tile_count, rows, width), f32)
    blocks = from_chip + from_cross[:1]
    out = call(
        functools.partial(rest_kernel, axis, chip_parts),
        "residual",
        [resident, *blocks],
        [vmem()] * (1 + len(blocks)),
        out_shape=shape,
        out_specs=hbm(),
        scratch_shapes=[
            pltpu.VMEM((2 * HALO, rows, width), f32),
            pltpu.SemaphoreType.DMA((len(blocks),)),
        ],
    )
    for (begin, size), rim in zip(rim_chunks[1:], from_cross[1:]):
        out = call(
            functools.partial(last_kernel, axis, begin),
            "residual_last",
            [resident, rim, out],
            [vmem()] * 2 + [hbm()],
            out_shape=shape,
            out_specs=hbm(),
            scratch_shapes=[
                pltpu.VMEM((HALO, size, width), f32),
                pltpu.SemaphoreType.DMA((1,)),
            ],
            input_output_aliases={2: 0},
        )
    return out


def solution(mesh):
    return jax.shard_map(
        on_device,
        mesh=mesh,
        in_specs=(
            P(("parts", "own"), None, None),
            P(("parts", "own"), None, None),
            P(("parts", "own"), None),
        ),
        out_specs=P(("parts", "own"), None, None),
        check_vma=False,
    )
```
